768 devices in a mesh: dp: 24 (over z, core), row: 32 (over y, x).
Axes of the slice: x: 4, y: 8, z: 12, core: 2. Of those that a mesh axis runs over, the one named last changes fastest.
Arguments:
- user_table: bfloat16 [196608, 256], P('row'), may hold values from -1 to 1
- user_ids: int32 [3072, 32], P('dp'), may hold values from 0 to 196607
- item_features: bfloat16 [196608, 256], P(('dp', 'row')), may hold values from -6 to 6
- counts: int32 [32, 96], P('row'), may hold values from 1 to 512, 6144 in all within a row
- placement: int32 [32, 96], P('row'), may hold values from 0 to 95, each once within a row
- labels: int32 [196608], P(('dp', 'row')), may hold values 0 or 1
- w_hidden: bfloat16 [768, 1024], replicated, may hold values from -0.21875 to 0.21875
- bias: float32 [1024], replicated, may hold values from -3 to 3
- w_out: bfloat16 [1024], replicated, may hold values from -0.1875 to 0.1875
Outputs:
- table_grad: float32 [196608, 256], P(('row', 'dp'))
- item_grad: bfloat16 [196608, 256], P(('dp', 'row'))
The draws below stay inside these ranges and needn't reach their ends.
Inputs may be any that keep to these rules, and one draw needn't show every extreme that they name: `counts`: each row sums to 6144. `placement`: each row is a permutation.
All inputs are finite; a program needn't handle non-finite values. No bound on the sum of `labels` on one device may be relied on, other than what follows from the above.
Results may differ from the reference program's by a relative error of at most 0.006.
Values may be sent and summed in bfloat16 or wider, within the bound.
A program may use at most 32 MiB of HBM per device.

```python
import math
import jax
import jax.numpy as jnp
import numpy as np
from jax import lax

E = 256
H = 1024
BAG = 32
CAND_MOST = 512
ROWS_DEV = 6144
REQ_DEV = 4
CAND_DEV = 256
USER_ROWS = 196608
REQS = 3072
CANDS = 196608
N_DP = 24
N_ROW = 32


def draw_user_ids(key, part):
    key = jax.random.fold_in(key, 11)
    keys = jax.random.split(key, 7)
    group_ids = N_ROW * REQ_DEV * BAG
    groups = REQS // (N_ROW * REQ_DEV)
    spread_ids = jax.random.randint(keys[0], (REQS * BAG,), 0, USER_ROWS)
    hot_rows = jax.random.randint(keys[1], (64,), 0, USER_ROWS)
    hot_pick = jax.random.randint(keys[2], (REQS * BAG,), 0, 64)
    use_hot = jax.random.randint(keys[3], (REQS * BAG,), 0, 4) == 0
    mixed = jnp.where(use_hot, hot_rows[hot_pick], spread_ids).astype(jnp.int32)
    crowd_group = jax.random.randint(keys[4], (), 0, groups)
    crowd_shard = jax.random.randint(keys[5], (), 0, N_ROW)
    order = jax.random.permutation(keys[6], ROWS_DEV).astype(jnp.int32)
    local = order[jnp.arange(group_ids, dtype=jnp.int32) % ROWS_DEV]
    crowded = (crowd_shard * ROWS_DEV + local).astype(jnp.int32)
    by_group = mixed.reshape(groups, group_ids)
    chosen = (jnp.arange(groups, dtype=jnp.int32) == crowd_group)[:, None]
    result = jnp.where(chosen, crowded[None, :], by_group)
    return result.reshape(REQS, BAG).astype(jnp.int32)


def with_ends(values, key, smallest, top_value):
    dims = values.shape
    index_at = [jax.random.randint(jax.random.fold_in(key, axis), (), 0, dims[axis]) for axis in range(len(dims))]
    values = values.at[tuple(index_at)].set(smallest)
    longest = dims.index(max(dims))
    index_at[longest] = (index_at[longest] + 1) % dims[longest]
    return values.at[tuple(index_at)].set(top_value)


def levels(own_key, dims, shards, low, high):
    loudness = 1.0
    for position, shards_of in shards:
        heights = jax.random.uniform(jax.random.fold_in(jax.random.fold_in(own_key, 6), position), (shards_of,), jnp.float32, low / len(shards), high / len(shards))
        loudness = loudness * jnp.repeat(jnp.exp(heights), dims[position] // shards_of).reshape((-1,) + (1,) * (len(dims) - 1 - position))
    return loudness


def split_up(count, total, most, lean):
    loads = [(1 << 20) // math.isqrt(grade ** lean) + 1 for grade in range(2, count + 1)]
    rest, holding = total - most - (count - 1), [1] * (count - 1)
    while rest > 0:
        movable = [i for i in range(count - 1) if holding[i] < most]
        whole, remaining = sum([loads[i] for i in movable]), rest
        for i in movable:
            more = min(most - holding[i], max(1, remaining * loads[i] // whole), rest)
            holding[i] = holding[i] + more
            rest = rest - more
    return np.array([most] + holding)


def ragged_sizes(own_key, amount, total, limit, skew):
    if amount == 2:
        one = jax.random.randint(own_key, (), max(1, total - limit), min(limit, total - 1) + 1)
        return jnp.stack([one, total - one])
    lengths = jnp.asarray(split_up(amount, total, limit, skew), jnp.int32)
    couples = (amount - 1) // 2
    giver, receiver = lengths[1:1 + 2 * couples:2], lengths[2:2 + 2 * couples:2]
    margin = jnp.minimum(giver - 1, limit - receiver)
    moved = jax.random.randint(jax.random.fold_in(own_key, 1), (couples,), 0, 1 << 20) % (margin + 1)
    lengths = lengths.at[1:1 + 2 * couples:2].set(giver - moved).at[2:2 + 2 * couples:2].set(receiver + moved)
    return lengths[jax.random.permutation(jax.random.fold_in(own_key, 2), amount)]


def centred(rng, extent, scale, reach, cuts=(), kind=jnp.bfloat16):
    drawn = scale * jax.random.normal(rng, extent, jnp.float32)
    if cuts:
        drawn = drawn * levels(rng, extent, cuts, -0.22, 0.18)
    return jnp.clip(drawn, -reach, reach).astype(kind)


def setup_inputs(seed: int = 0) -> dict:
    splits = jax.random.split(jax.random.key(seed), 10)
    user_table = centred(splits[0], (USER_ROWS, E), 0.18, 1.0, ((0, 32),))
    user_ids = draw_user_ids(jax.random.fold_in(splits[9], 71), 0)
    item_features = centred(splits[2], (CANDS, E), 1.0, 6.0, ((0, 768),))
    counts = jax.vmap(lambda own: ragged_sizes(own, N_DP * REQ_DEV, N_DP * CAND_DEV, CAND_MOST, 2))(jax.random.split(splits[3], N_ROW)).reshape((N_ROW, N_DP * REQ_DEV)).astype(jnp.int32)
    placement = jax.vmap(lambda own: jax.random.permutation(own, N_DP * REQ_DEV))(jax.random.split(splits[4], N_ROW)).reshape((N_ROW, N_DP * REQ_DEV)).astype(jnp.int32)
    labels = with_ends((jax.random.randint(splits[5], (CANDS,), 0, 2) < 1).astype(jnp.int32), jax.random.fold_in(splits[5], 1), 0, 1)
    w_hidden = centred(splits[6], (3 * E, H), (3 * E) ** -0.5, 0.21875)
    bias = centred(splits[7], (H,), 0.5, 3.0, (), jnp.float32)
    w_out = centred(splits[8], (H,), H ** -0.5, 0.1875)
    return {"user_table": user_table, "user_ids": user_ids, "item_features": item_features, "counts": counts, "placement": placement, "labels": labels, "w_hidden": w_hidden, "bias": bias, "w_out": w_out}


def column_owner(column_counts, order):
    total = N_DP * REQ_DEV
    ordered = jnp.take(column_counts, order)
    before = (jnp.cumsum(ordered) - ordered).astype(jnp.int32)
    starts = jnp.zeros((total,), jnp.int32).at[order].set(before)
    slots = jnp.arange(N_DP * CAND_DEV, dtype=jnp.int32)
    inside = (slots[:, None] >= starts[None, :]) & (slots[:, None] < (starts + column_counts)[None, :])
    index = jnp.arange(total, dtype=jnp.int32)
    return jnp.sum(jnp.where(inside, index[None, :], 0), axis=1).astype(jnp.int32)


def score_block(user_rows, item_features, labels, w_hidden, bias, w_out):
    both = (user_rows.astype(jnp.float32) * item_features.astype(jnp.float32)).astype(jnp.bfloat16)
    features = jnp.concatenate([user_rows, item_features, both], axis=1)
    pre = jnp.dot(features, w_hidden, preferred_element_type=jnp.float32) + bias
    hidden = jax.nn.silu(pre).astype(jnp.bfloat16)
    score = jnp.dot(hidden, w_out, preferred_element_type=jnp.float32)
    dscore = 64.0 * (jax.nn.sigmoid(score) - labels.astype(jnp.float32))
    sigma = jax.nn.sigmoid(pre)
    slope = sigma * (1.0 + pre * (1.0 - sigma))
    dhidden = (dscore[:, None] * w_out.astype(jnp.float32)[None, :] * slope).astype(jnp.bfloat16)
    dfeatures = lax.dot_general(dhidden, w_hidden, (((1,), (1,)), ((), ())), preferred_element_type=jnp.float32)
    item_grad = (dfeatures[:, E:2 * E] + dfeatures[:, 2 * E:] * user_rows.astype(jnp.float32)).astype(jnp.bfloat16)
    user_grad = dfeatures[:, :E] + dfeatures[:, 2 * E:] * item_features.astype(jnp.float32)
    return item_grad, user_grad


def reference(user_table, user_ids, item_features, counts, placement, labels, w_hidden, bias, w_out):
    owner_column = jax.vmap(column_owner)(counts, placement)
    column_index = jnp.arange(N_ROW, dtype=jnp.int32)[:, None]
    owner_global = ((owner_column // REQ_DEV) * N_ROW + column_index) * REQ_DEV + owner_column % REQ_DEV
    owner = owner_global.reshape(N_ROW, N_DP, CAND_DEV).transpose(1, 0, 2).reshape(-1)
    pooled = jnp.sum(user_table[user_ids].astype(jnp.float32), axis=1).astype(jnp.bfloat16)
    user_rows = pooled[owner]
    blocks = N_DP

    def run(packed):
        return score_block(packed[0], packed[1], packed[2], w_hidden, bias, w_out)

    item_grad, user_grad = lax.map(run, (user_rows.reshape(blocks, -1, E), item_features.reshape(blocks, -1, E), labels.reshape(blocks, -1)))
    item_grad = item_grad.reshape(-1, E)
    user_grad = user_grad.reshape(-1, E)
    request_grad = jax.ops.segment_sum(user_grad, owner, num_segments=REQS)
    spread = jnp.repeat(request_grad, BAG, axis=0)
    table_grad = jax.ops.segment_sum(spread, user_ids.reshape(-1), num_segments=USER_ROWS)
    return table_grad, item_grad
```

```python
import functools

import jax
import jax.numpy as jnp
from jax import lax
from jax.experimental import pallas as pl
from jax.experimental.pallas import tpu as pltpu
from jax.sharding import PartitionSpec as P

MESH = pl.DeviceIdType.MESH
loss_scale = 64.0

N_DP = 24
N_ROW = 32
N_X = 4
N_Z = 12
REQ = 4
GROUP = N_ROW * REQ
COLUMN = N_DP * REQ
BAG = 32
E = 256
H = 1024
ROWS = 6144
SHARE = ROWS // N_DP
CAND = 256
QUARTER = GROUP // N_X
BLOCK = 16
N_BLOCK = GROUP // BLOCK
BF16 = jnp.bfloat16
F32 = jnp.float32


def iota(shape, dim, dtype=jnp.int32):
    return lax.broadcasted_iota(jnp.int32, shape, dim).astype(dtype)


def to_messages(rows):
    n = rows.shape[0] // 8
    left = rows[:, :128].reshape(n, 8, 128)
    right = rows[:, 128:].reshape(n, 8, 128)
    upper = iota((n, 8, 128), 1) < 4
    even = jnp.where(upper, left, pltpu.roll(right, 4, axis=1))
    odd = jnp.where(upper, pltpu.roll(left, 4, axis=1), right)
    return jnp.stack([even, odd], axis=1).reshape(2 * n, 8, 128)


def from_messages(messages):
    n = messages.shape[0] // 2
    pairs = messages.reshape(n, 2, 8, 128)
    even, odd = pairs[:, 0], pairs[:, 1]
    upper = iota((n, 8, 128), 1) < 4
    left = jnp.where(upper, even, pltpu.roll(odd, 4, axis=1))
    right = jnp.where(upper, pltpu.roll(even, 4, axis=1), odd)
    return left.reshape(8 * n, 128), right.reshape(8 * n, 128)


def kernel(
    table_hbm,
    ids_flat_ref,
    ids_turned_ref,
    item_ref,
    counts_ref,
    placement_ref,
    labels_ref,
    w_hidden_hbm,
    bias_ref,
    w_out_ref,
    table_grad_ref,
    item_grad_ref,
    table,
    w_hidden,
    group_counts,
    partial_out,
    partial_in,
    pooled_out,
    pooled_in,
    pooled_column,
    grad_out,
    grad_in,
    request_out,
    request_in,
    ids_all,
    own_counts,
    all_grads,
    load_sem,
    ids_send,
    ids_recv,
    partial_send,
    partial_recv,
    pooled_send,
    pooled_recv,
    grad_send,
    grad_recv,
    request_send,
    request_recv,
    z_send,
    z_recv,
    x_send,
    x_recv,
    core_send,
    core_recv,
):
    i = lax.axis_index("dp")
    k = lax.axis_index("row")
    z = i // 2
    core = i % 2
    y = k // N_X
    x = k % N_X

    table_load = pltpu.make_async_copy(table_hbm, table, load_sem.at[0])
    table_load.start()
    w_load = pltpu.make_async_copy(w_hidden_hbm, w_hidden, load_sem.at[1])
    w_load.start()

    barrier = pltpu.get_barrier_semaphore()

    def greet_row(s, _):
        pl.semaphore_signal(barrier, inc=1, device_id=(i, (k + s) % N_ROW), device_id_type=MESH)
        return 0

    def greet_dp(s, _):
        pl.semaphore_signal(barrier, inc=1, device_id=((i + s) % N_DP, k), device_id_type=MESH)
        return 0

    lax.fori_loop(1, N_ROW, greet_row, 0)
    lax.fori_loop(1, N_DP, greet_dp, 0)

    relative = ids_flat_ref[...] - k * ROWS
    inside = (relative >= 0) & (relative < ROWS)
    in_block = iota((N_BLOCK, BLOCK * BAG), 1) // BAG
    high_key = jnp.where(inside, (relative // SHARE) * BLOCK + in_block, -1)
    low_key = relative % SHARE
    high_row = iota((N_DP * BLOCK, 1), 0)
    low_row = iota((SHARE, 1), 0)
    for b in range(N_BLOCK):
        high = jnp.where(high_key[b : b + 1] == high_row, 1.0, 0.0).astype(BF16)
        low = jnp.where(low_key[b : b + 1] == low_row, 1.0, 0.0).astype(BF16)
        found = lax.dot_general(high, low, (((1,), (1,)), ((), ())), preferred_element_type=F32).astype(BF16)
        for h in range(N_DP):
            group_counts[b * BLOCK : (b + 1) * BLOCK, h * SHARE : (h + 1) * SHARE] = found[
                h * BLOCK : (h + 1) * BLOCK
            ]
    table_load.wait()
    partial = jnp.dot(group_counts[...], table[...], preferred_element_type=F32)
    partial_out[...] = to_messages(partial)

    pl.semaphore_wait(barrier, N_ROW - 1 + N_DP - 1)

    def row_copy(src, dst, send, recv, s):
        return pltpu.make_async_remote_copy(
            src_ref=src,
            dst_ref=dst,
            send_sem=send.at[s],
            recv_sem=recv.at[k],
            device_id=(i, (k + s) % N_ROW),
            device_id_type=MESH,
        )

    def dp_copy(src, dst, send, recv, s):
        return pltpu.make_async_remote_copy(
            src_ref=src,
            dst_ref=dst,
            send_sem=send.at[s],
            recv_sem=recv.at[i],
            device_id=((i + s) % N_DP, k),
            device_id_type=MESH,
        )

    def arrived(buffer, recv, source):
        pltpu.make_async_copy(buffer.at[source], buffer.at[source], recv.at[source]).wait()

    def send_partial(s, _):
        row_copy(partial_out.at[(k + s) % N_ROW], partial_in.at[k], partial_send, partial_recv, s).start()
        return 0

    lax.fori_loop(1, N_ROW, send_partial, 0)
    partial_in[k] = partial_out[k]

    ids_all[i] = ids_turned_ref[...]

    def send_ids(s, _):
        dp_copy(ids_turned_ref, ids_all.at[i], ids_send, ids_recv, s).start()
        return 0

    lax.fori_loop(1, N_DP, send_ids, 0)

    order = placement_ref[...]
    column_counts = counts_ref[...]
    eye = iota((128, 128), 0) == iota((128, 128), 1)
    place_at = jnp.where(order == iota((128, 128), 0), iota((128, 128), 1).astype(F32), 0.0)
    position = jnp.sum(place_at, axis=1, keepdims=True)
    position_row = jnp.sum(jnp.where(eye, position, 0.0), axis=0, keepdims=True)
    start = jnp.sum(jnp.where(position_row < position, column_counts, 0.0), axis=1, keepdims=True)
    count = jnp.sum(jnp.where(eye, column_counts, 0.0), axis=1, keepdims=True)
    start_row = jnp.sum(jnp.where(eye, start, 0.0), axis=0, keepdims=True)
    end, end_row = start + count, start_row + column_counts
    first = (i * CAND).astype(F32)
    slot = first + iota((CAND, 1), 0, F32)
    slot_row = first + iota((1, CAND), 1, F32)
    member = jnp.where((slot >= start_row) & (slot < end_row), 1.0, 0.0).astype(BF16)
    member_turned = jnp.where((slot_row >= start) & (slot_row < end), 1.0, 0.0).astype(BF16)
    diagonal = iota((CAND, CAND), 0) == iota((CAND, CAND), 1)
    label = jnp.sum(jnp.where(diagonal, labels_ref[...].astype(F32), 0.0), axis=1, keepdims=True)

    item = item_ref[...]
    item_wide = item.astype(F32)
    w_load.wait()
    item_pre = jnp.dot(item, w_hidden[E : 2 * E], preferred_element_type=F32) + bias_ref[...]

    def wait_partial(s, _):
        arrived(partial_in, partial_recv, (k + s) % N_ROW)
        return 0

    lax.fori_loop(1, N_ROW, wait_partial, 0)
    pooled = jnp.sum(partial_in[...], axis=0)
    pooled_out[...] = pooled
    pooled_in[i] = pooled

    def send_pooled(s, _):
        dp_copy(pooled_out, pooled_in.at[i], pooled_send, pooled_recv, s).start()
        return 0

    def wait_pooled(s, _):
        arrived(pooled_in, pooled_recv, (i + s) % N_DP)
        return 0

    lax.fori_loop(1, N_DP, send_pooled, 0)
    pooled_column[...] = jnp.zeros_like(pooled_column)
    lax.fori_loop(1, N_DP, wait_pooled, 0)
    left, right = from_messages(pooled_in[...])
    pooled_column[:COLUMN, :128] = left.astype(BF16)
    pooled_column[:COLUMN, 128:] = right.astype(BF16)

    user_rows = jnp.dot(member, pooled_column[...], preferred_element_type=F32)
    user = user_rows.astype(BF16)
    both = (user_rows * item_wide).astype(BF16)
    pre = (
        item_pre
        + jnp.dot(user, w_hidden[:E], preferred_element_type=F32)
        + jnp.dot(both, w_hidden[2 * E :], preferred_element_type=F32)
    )
    sigma = jax.nn.sigmoid(pre)
    hidden = (pre * sigma).astype(BF16).astype(F32)
    w_out = w_out_ref[...].astype(F32)
    score = jnp.sum(hidden * w_out, axis=1, keepdims=True)
    dscore = loss_scale * (jax.nn.sigmoid(score) - label)
    slope = sigma * (1.0 + pre * (1.0 - sigma))
    dhidden = (dscore * w_out * slope).astype(BF16)
    dfeatures = lax.dot_general(dhidden, w_hidden[...], (((1,), (1,)), ((), ())), preferred_element_type=F32)
    item_grad_ref[...] = (dfeatures[:, E : 2 * E] + dfeatures[:, 2 * E :] * user_rows).astype(BF16)
    user_grad = dfeatures[:, :E] + dfeatures[:, 2 * E :] * item_wide
    coarse = user_grad.astype(BF16)
    fine = (user_grad - coarse.astype(F32)).astype(BF16)
    column_grad = jnp.dot(member_turned, coarse, preferred_element_type=F32) + jnp.dot(
        member_turned, fine, preferred_element_type=F32
    )
    grad_out[...] = to_messages(column_grad[:COLUMN])

    def send_grad(s, _):
        dp_copy(grad_out.at[(i + s) % N_DP], grad_in.at[i], grad_send, grad_recv, s).start()
        return 0

    def wait_grad(s, _):
        arrived(grad_in, grad_recv, (i + s) % N_DP)
        return 0

    lax.fori_loop(1, N_DP, send_grad, 0)
    grad_in[i] = grad_out[i]
    lax.fori_loop(1, N_DP, wait_grad, 0)
    request_grad = jnp.sum(grad_in[...], axis=0)
    request_out[...] = request_grad
    request_in[k] = request_grad

    def send_request(s, _):
        row_copy(request_out, request_in.at[k], request_send, request_recv, s).start()
        return 0

    def wait_request(s, _):
        arrived(request_in, request_recv, (k + s) % N_ROW)
        return 0

    lax.fori_loop(1, N_ROW, send_request, 0)
    lax.fori_loop(1, N_ROW, wait_request, 0)
    left, right = from_messages(request_in[...])
    all_grads[z, core, :, :128] = left.astype(BF16)
    all_grads[z, core, :, 128:] = right.astype(BF16)

    def quarter(where, which):
        return all_grads.at[where, core, pl.ds(pl.multiple_of(which * QUARTER, QUARTER), QUARTER)]

    def send_z(s, _):
        pltpu.make_async_remote_copy(
            src_ref=quarter(z, x),
            dst_ref=quarter(z, x),
            send_sem=z_send.at[s],
            recv_sem=z_recv.at[z],
            device_id=(((z + s) % N_Z) * 2 + core, k),
            device_id_type=MESH,
        ).start()
        return 0

    lax.fori_loop(1, N_Z, send_z, 0)

    def x_copy(where, which, s):
        return pltpu.make_async_remote_copy(
            src_ref=quarter(where, which),
            dst_ref=quarter(where, which),
            send_sem=x_send.at[where, s],
            recv_sem=x_recv.at[where, which],
            device_id=(i, y * N_X + (x + s) % N_X),
            device_id_type=MESH,
        )

    def core_copy(where, side):
        return pltpu.make_async_remote_copy(
            src_ref=all_grads.at[where, side],
            dst_ref=all_grads.at[where, side],
            send_sem=core_send.at[where],
            recv_sem=core_recv.at[where],
            device_id=(z * 2 + 1 - core, k),
            device_id_type=MESH,
        )

    core_copy(z, core).start()

    own_first = k * ROWS + i * SHARE

    def count_group(group):
        ids = ids_all[group] - own_first
        row = iota((SHARE, GROUP), 0)
        total = jnp.zeros((SHARE, GROUP), F32)
        for b in range(BAG):
            total = total + jnp.where(ids[b : b + 1] == row, 1.0, 0.0)
        columns = pl.ds(pl.multiple_of(group * GROUP, GROUP), GROUP)
        own_counts[:, columns] = total.astype(BF16)

    def wait_ids(s, _):
        arrived(ids_all, ids_recv, (i + s) % N_DP)
        return 0

    lax.fori_loop(1, N_DP, wait_ids, 0)

    def pass_on(s, _):
        where = (z + s) % N_Z
        block = quarter(where, x)
        pltpu.make_async_copy(block, block, z_recv.at[where]).wait()
        for step in range(1, N_X):
            x_copy(where, x, step).start()
        count_group(2 * s)
        count_group(2 * s + 1)
        return 0

    lax.fori_loop(1, N_Z, pass_on, 0)
    count_group(0)
    count_group(1)

    def to_other_core(s, _):
        where = (z + s) % N_Z
        for step in range(1, N_X):
            which = (x + step) % N_X
            block = quarter(where, which)
            pltpu.make_async_copy(block, block, x_recv.at[where, which]).wait()
        core_copy(where, core).start()
        return 0

    lax.fori_loop(1, N_Z, to_other_core, 0)

    def wait_core(where, _):
        block = all_grads.at[where, 1 - core]
        pltpu.make_async_copy(block, block, core_recv.at[where]).wait()
        return 0

    lax.fori_loop(0, N_Z, wait_core, 0)
    table_grad_ref[...] = jnp.dot(
        own_counts[...], all_grads[...].reshape(N_DP * GROUP, E), preferred_element_type=F32
    )

    def drain_row(s, _):
        row_copy(partial_out.at[0], partial_in.at[k], partial_send, partial_recv, s).wait_send()
        row_copy(request_out, request_in.at[k], request_send, request_recv, s).wait_send()
        return 0

    def drain_dp(s, _):
        dp_copy(ids_turned_ref, ids_all.at[i], ids_send, ids_recv, s).wait_send()
        dp_copy(pooled_out, pooled_in.at[i], pooled_send, pooled_recv, s).wait_send()
        dp_copy(grad_out.at[0], grad_in.at[i], grad_send, grad_recv, s).wait_send()
        return 0

    def drain_z(s, _):
        block = quarter(z, x)
        pltpu.make_async_copy(block, block, z_send.at[s]).wait()
        where = (z + s) % N_Z
        for step in range(1, N_X):
            x_copy(where, x, step).wait_send()
        core_copy(where, core).wait_send()
        return 0

    lax.fori_loop(1, N_ROW, drain_row, 0)
    lax.fori_loop(1, N_DP, drain_dp, 0)
    lax.fori_loop(1, N_Z, drain_z, 0)
    core_copy(z, core).wait_send()


def per_device(user_table, user_ids, item_features, counts, placement, labels, w_hidden, bias, w_out):
    ids_flat = user_ids.reshape(N_BLOCK, BLOCK * BAG)
    ids_turned = user_ids.T
    pad = ((0, 0), (0, 128 - COLUMN))
    counts_row = jnp.pad(counts.astype(F32), pad)
    placement_row = jnp.pad(placement, pad, constant_values=-1)
    vmem = pl.BlockSpec(memory_space=pltpu.VMEM)
    hbm = pl.BlockSpec(memory_space=pl.ANY)
    dma = pltpu.SemaphoreType.DMA
    return pl.pallas_call(
        kernel,
        out_shape=(
            jax.ShapeDtypeStruct((SHARE, E), F32),
            jax.ShapeDtypeStruct((CAND, E), BF16),
        ),
        in_specs=[hbm, vmem, vmem, vmem, vmem, vmem, vmem, hbm, vmem, vmem],
        out_specs=(vmem, vmem),
        scratch_shapes=[
            pltpu.VMEM((ROWS, E), BF16),
            pltpu.VMEM((3 * E, H), BF16),
            pltpu.VMEM((GROUP, ROWS), BF16),
            pltpu.VMEM((N_ROW, 8, 128), F32),
            pltpu.VMEM((N_ROW, 8, 128), F32),
            pltpu.VMEM((8, 128), F32),
            pltpu.VMEM((N_DP, 8, 128), F32),
            pltpu.VMEM((128, E), BF16),
            pltpu.VMEM((N_DP, 8, 128), F32),
            pltpu.VMEM((N_DP, 8, 128), F32),
            pltpu.VMEM((8, 128), F32),
            pltpu.VMEM((N_ROW, 8, 128), F32),
            pltpu.VMEM((N_DP, BAG, GROUP), jnp.int32),
            pltpu.VMEM((SHARE, N_DP * GROUP), BF16),
            pltpu.VMEM((N_Z, 2, GROUP, E), BF16),
            dma((2,)),
            dma((N_DP,)),
            dma((N_DP,)),
            dma((N_ROW,)),
            dma((N_ROW,)),
            dma((N_DP,)),
            dma((N_DP,)),
            dma((N_DP,)),
            dma((N_DP,)),
            dma((N_ROW,)),
            dma((N_ROW,)),
            dma((N_Z,)),
            dma((N_Z,)),
            dma((N_Z, N_X)),
            dma((N_Z, N_X)),
            dma((N_Z,)),
            dma((N_Z,)),
        ],
        compiler_params=pltpu.CompilerParams(
            collective_id=0, has_side_effects=True, vmem_limit_bytes=48 * 1024 * 1024
        ),
    )(
        user_table,
        ids_flat,
        ids_turned,
        item_features,
        counts_row,
        placement_row,
        labels.reshape(1, CAND),
        w_hidden,
        bias.reshape(1, H),
        w_out.reshape(1, H),
    )


def solution(mesh):
    return jax.shard_map(
        per_device,
        mesh=mesh,
        in_specs=(
            P("row", None),
            P("dp", None),
            P(("dp", "row"), None),
            P("row", None),
            P("row", None),
            P(("dp", "row")),
            P(),
            P(),
            P(),
        ),
        out_specs=(P(("row", "dp"), None), P(("dp", "row"), None)),
        check_vma=False,
    )
```

```python
import functools

import jax
import jax.numpy as jnp
from jax import lax
from jax.experimental import pallas as pl
from jax.experimental.pallas import tpu as pltpu
from jax.sharding import PartitionSpec as P

MESH = pl.DeviceIdType.MESH
loss_scale = 64.0

N_DP = 24
N_ROW = 32
N_X = 4
N_Z = 12
REQ = 4
GROUP = N_ROW * REQ
COLUMN = N_DP * REQ
BAG = 32
E = 256
H = 1024
ROWS = 6144
SHARE = ROWS // N_DP
CAND = 256
QUARTER = GROUP // N_X
N_Y = N_ROW // N_X
BLOCK = 16
N_BLOCK = GROUP // BLOCK
BF16 = jnp.bfloat16
F32 = jnp.float32


def iota(shape, dim, dtype=jnp.int32):
    return lax.broadcasted_iota(jnp.int32, shape, dim).astype(dtype)


def to_messages(rows):
    n = rows.shape[0] // 8
    left = rows[:, :128].reshape(n, 8, 128)
    right = rows[:, 128:].reshape(n, 8, 128)
    upper = iota((n, 8, 128), 1) < 4
    even = jnp.where(upper, left, pltpu.roll(right, 4, axis=1))
    odd = jnp.where(upper, pltpu.roll(left, 4, axis=1), right)
    return jnp.stack([even, odd], axis=1).reshape(2 * n, 8, 128)


def from_messages(messages):
    n = messages.shape[0] // 2
    pairs = messages.reshape(n, 2, 8, 128)
    even, odd = pairs[:, 0], pairs[:, 1]
    upper = iota((n, 8, 128), 1) < 4
    left = jnp.where(upper, even, pltpu.roll(odd, 4, axis=1))
    right = jnp.where(upper, pltpu.roll(even, 4, axis=1), odd)
    return left.reshape(8 * n, 128), right.reshape(8 * n, 128)


def wrap(value, size):
    return jnp.where(value >= size, value - size, value)


def alternate(s, size):
    half = (s + 1) // 2
    return jnp.where(s % 2 == 1, half, wrap(size - half, size))


def flatten(turned):
    lag = (iota((8, 128), 0) + 8 - iota((8, 128), 1) // BLOCK) % 8
    parts = []
    for first in range(0, BAG, 8):
        tile = turned[first : first + 8]
        part = tile
        for d in range(1, 8):
            moved = pltpu.roll(pltpu.roll(tile, d, axis=0), 128 - BLOCK * d, axis=1)
            part = jnp.where(lag == d, moved, part)
        parts.append(part)
    return jnp.concatenate(parts, axis=1)


def kernel(
    table_hbm,
    ids_hbm,
    item_hbm,
    counts_hbm,
    placement_hbm,
    labels_hbm,
    w_hidden_hbm,
    bias_hbm,
    w_out_ref,
    table_grad_ref,
    item_grad_ref,
    table,
    w_hidden,
    ids_ref,
    item_ref,
    counts_ref,
    placement_ref,
    labels_ref,
    bias_ref,
    group_counts,
    partial_out,
    partial_in,
    pooled_out,
    pooled_in,
    pooled_column,
    grad_out,
    grad_core,
    grad_pair,
    grad_in,
    request_out,
    request_in,
    ids_all,
    own_counts,
    all_grads,
    load_sem,
    ids_send,
    ids_recv,
    partial_send,
    partial_recv,
    pooled_send,
    pooled_recv,
    grad_send,
    grad_recv,
    request_send,
    request_recv,
    z_send,
    z_recv,
    x_send,
    x_recv,
    core_send,
    core_recv,
):
    i = lax.axis_index("dp")
    k = lax.axis_index("row")
    z = i // 2
    core = i % 2
    y = k // N_X
    x = k % N_X

    ids_load = pltpu.make_async_copy(ids_hbm, ids_ref, load_sem.at[0])
    table_load = pltpu.make_async_copy(table_hbm, table, load_sem.at[1])
    later_loads = [
        pltpu.make_async_copy(source, target, load_sem.at[n])
        for n, (source, target) in enumerate(
            [
                (placement_hbm, placement_ref),
                (counts_hbm, counts_ref),
                (labels_hbm, labels_ref),
                (item_hbm, item_ref),
                (bias_hbm, bias_ref),
                (w_hidden_hbm, w_hidden),
            ],
            2,
        )
    ]
    ids_load.start()
    table_load.start()
    for load in later_loads:
        load.start()

    barrier = pltpu.get_barrier_semaphore()

    def greet_row(s, _):
        pl.semaphore_signal(barrier, inc=1, device_id=(i, (k + s) % N_ROW), device_id_type=MESH)
        return 0

    def greet_z(s, _):
        there = wrap(z + s, N_Z) * 2 + core
        pl.semaphore_signal(barrier, inc=1, device_id=(there, k), device_id_type=MESH)
        return 0

    lax.fori_loop(1, N_ROW, greet_row, 0)
    lax.fori_loop(1, N_Z, greet_z, 0)
    pl.semaphore_signal(barrier, inc=1, device_id=(z * 2 + 1 - core, k), device_id_type=MESH)

    ids_load.wait()
    relative = ids_ref[...] - k * ROWS
    relative = jnp.where((relative >= 0) & (relative < ROWS), relative, -1)
    flat = flatten(relative)
    in_block = iota((N_BLOCK, BLOCK * BAG), 1) % BLOCK
    high_key = jnp.where(flat >= 0, (flat >> 8) * BLOCK + in_block, -1)
    low_key = flat & (SHARE - 1)
    high_row = iota((N_DP * BLOCK, 1), 0)
    low_row = iota((SHARE, 1), 0)
    for b in range(N_BLOCK):
        high = jnp.where(high_key[b : b + 1] == high_row, 1.0, 0.0).astype(BF16)
        low = jnp.where(low_key[b : b + 1] == low_row, 1.0, 0.0).astype(BF16)
        found = lax.dot_general(high, low, (((1,), (1,)), ((), ())), preferred_element_type=F32).astype(BF16)
        for h in range(N_DP):
            group_counts[b * BLOCK : (b + 1) * BLOCK, h * SHARE : (h + 1) * SHARE] = found[
                h * BLOCK : (h + 1) * BLOCK
            ]
    table_load.wait()
    partial = jnp.dot(group_counts[...], table[...], preferred_element_type=F32)
    partial_out[...] = to_messages(partial)

    pl.semaphore_wait(barrier, N_ROW - 1 + N_Z)

    def row_copy(src, dst, send, recv, s):
        return pltpu.make_async_remote_copy(
            src_ref=src,
            dst_ref=dst,
            send_sem=send.at[s],
            recv_sem=recv.at[k],
            device_id=(i, (k + s) % N_ROW),
            device_id_type=MESH,
        )

    def z_copy(src, dst, send, recv, s):
        return pltpu.make_async_remote_copy(
            src_ref=src,
            dst_ref=dst,
            send_sem=send.at[s],
            recv_sem=recv.at[z],
            device_id=(wrap(z + s, N_Z) * 2 + core, k),
            device_id_type=MESH,
        )

    def core_copy(src, dst, n):
        return pltpu.make_async_remote_copy(
            src_ref=src,
            dst_ref=dst,
            send_sem=core_send.at[n],
            recv_sem=core_recv.at[n],
            device_id=(z * 2 + 1 - core, k),
            device_id_type=MESH,
        )

    def arrived(buffer, recv, source):
        pltpu.make_async_copy(buffer.at[source], buffer.at[source], recv.at[source]).wait()

    def send_partial(s, _):
        row_copy(partial_out.at[(k + s) % N_ROW], partial_in.at[k], partial_send, partial_recv, s).start()
        return 0

    lax.fori_loop(1, N_ROW, send_partial, 0)
    partial_in[k] = partial_out[k]

    to = iota((GROUP, GROUP), 1)
    moved_from = (to % QUARTER // REQ) * (N_X * REQ) + to // QUARTER * REQ + to % REQ
    reorder = jnp.where(iota((GROUP, GROUP), 0) == moved_from, 1.0, 0.0).astype(BF16)
    high_digit = (relative >> 8).astype(F32).astype(BF16)
    low_digit = (relative & (SHARE - 1)).astype(F32).astype(BF16)
    ids_moved = jnp.dot(high_digit, reorder, preferred_element_type=F32) * SHARE + jnp.dot(
        low_digit, reorder, preferred_element_type=F32
    )
    ids_all[core, z] = ids_moved.astype(jnp.int32).astype(jnp.int16)

    def send_ids(s, _):
        z_copy(ids_all.at[core, z], ids_all.at[core, z], ids_send, ids_recv, alternate(s, N_Z)).start()
        return 0

    lax.fori_loop(1, N_Z, send_ids, 0)

    own_first = i * SHARE

    def count_group(side, where):
        ids = jnp.clip(ids_all[side, where].astype(jnp.int32) - own_first, -1, SHARE).astype(F32)
        row = iota((SHARE, GROUP), 0, F32).astype(BF16)
        total = jnp.zeros((SHARE, GROUP), BF16)
        one, zero = jnp.ones((), BF16), jnp.zeros((), BF16)
        for b in range(BAG):
            wanted = jnp.broadcast_to(ids[b : b + 1], (16, GROUP)).astype(BF16)
            total = total + jnp.where(jnp.tile(wanted, (SHARE // 16, 1)) == row, one, zero)
        columns = pl.ds(pl.multiple_of((side * N_Z + where) * GROUP, GROUP), GROUP)
        own_counts[:, columns] = total

    def count_own_core(s, _):
        count_group(core, wrap(z + alternate(s, N_Z), N_Z))
        return 0

    def count_other_core(where, _):
        count_group(1 - core, where)
        return 0

    for load in later_loads:
        load.wait()
    padding = jnp.zeros((1, 128 - COLUMN), jnp.int32)
    order = jnp.concatenate([placement_ref[...], padding - 1], axis=1)
    column_counts = jnp.concatenate([counts_ref[...], padding], axis=1).astype(F32)
    eye = iota((128, 128), 0) == iota((128, 128), 1)
    place_at = jnp.where(order == iota((128, 128), 0), iota((128, 128), 1).astype(F32), 0.0)
    position = jnp.sum(place_at, axis=1, keepdims=True)
    position_row = jnp.sum(jnp.where(eye, position, 0.0), axis=0, keepdims=True)
    start = jnp.sum(jnp.where(position_row < position, column_counts, 0.0), axis=1, keepdims=True)
    count = jnp.sum(jnp.where(eye, column_counts, 0.0), axis=1, keepdims=True)
    start_row = jnp.sum(jnp.where(eye, start, 0.0), axis=0, keepdims=True)
    end, end_row = start + count, start_row + column_counts
    first = (i * CAND).astype(F32)
    slot = first + iota((CAND, 1), 0, F32)
    slot_row = first + iota((1, CAND), 1, F32)
    member = jnp.where((slot >= start_row) & (slot < end_row), 1.0, 0.0).astype(BF16)
    member_turned = jnp.where((slot_row >= start) & (slot_row < end), 1.0, 0.0).astype(BF16)
    diagonal = iota((CAND, CAND), 0) == iota((CAND, CAND), 1)
    label = jnp.sum(jnp.where(diagonal, labels_ref[...].astype(F32), 0.0), axis=1, keepdims=True)

    item = item_ref[...]
    item_wide = item.astype(F32)
    item_pre = jnp.dot(item, w_hidden[E : 2 * E], preferred_element_type=F32) + bias_ref[...]

    count_group(core, z)

    def wait_partial(s, _):
        arrived(partial_in, partial_recv, (k + s) % N_ROW)
        return 0

    lax.fori_loop(1, N_ROW, wait_partial, 0)
    pooled = jnp.sum(partial_in[...], axis=0)
    pooled_out[...] = pooled
    pooled_in[core, z] = pooled

    def send_pooled(s, _):
        z_copy(pooled_out, pooled_in.at[core, z], pooled_send, pooled_recv, alternate(s, N_Z)).start()
        return 0

    def wait_ids(s, _):
        where = wrap(z + s, N_Z)
        block = ids_all.at[core, where]
        pltpu.make_async_copy(block, block, ids_recv.at[where]).wait()
        return 0

    def wait_pooled(s, _):
        where = wrap(z + s, N_Z)
        block = pooled_in.at[core, where]
        pltpu.make_async_copy(block, block, pooled_recv.at[where]).wait()
        return 0

    lax.fori_loop(1, N_Z, send_pooled, 0)
    pooled_column[...] = jnp.zeros_like(pooled_column)
    lax.fori_loop(1, N_Z, wait_ids, 0)
    ids_over = core_copy(ids_all.at[core], ids_all.at[core], 0)
    ids_over.start()
    lax.fori_loop(1, 8, count_own_core, 0)
    lax.fori_loop(1, N_Z, wait_pooled, 0)
    pooled_over = core_copy(pooled_in.at[core], pooled_in.at[core], 1)
    pooled_over.start()
    pooled_over.wait_recv()
    pooled_all = jnp.stack([pooled_in[0], pooled_in[1]], axis=1).reshape(N_DP, 8, 128)
    left, right = from_messages(pooled_all)
    pooled_column[:COLUMN, :128] = left.astype(BF16)
    pooled_column[:COLUMN, 128:] = right.astype(BF16)

    user_rows = jnp.dot(member, pooled_column[...], preferred_element_type=F32)
    user = user_rows.astype(BF16)
    both = (user_rows * item_wide).astype(BF16)
    pre = (
        item_pre
        + jnp.dot(user, w_hidden[:E], preferred_element_type=F32)
        + jnp.dot(both, w_hidden[2 * E :], preferred_element_type=F32)
    )
    sigma = jax.nn.sigmoid(pre)
    hidden = (pre * sigma).astype(BF16).astype(F32)
    w_out = w_out_ref[...].astype(F32).reshape(1, H)
    score = jnp.sum(hidden * w_out, axis=1, keepdims=True)
    dscore = loss_scale * (jax.nn.sigmoid(score) - label)
    slope = sigma * (1.0 + pre * (1.0 - sigma))
    dhidden = (dscore * w_out * slope).astype(BF16)
    dfeatures = lax.dot_general(dhidden, w_hidden[...], (((1,), (1,)), ((), ())), preferred_element_type=F32)
    user_grad = dfeatures[:, :E] + dfeatures[:, 2 * E :] * item_wide
    coarse = user_grad.astype(BF16)
    fine = (user_grad - coarse.astype(F32)).astype(BF16)
    column_grad = jnp.dot(member_turned, coarse, preferred_element_type=F32) + jnp.dot(
        member_turned, fine, preferred_element_type=F32
    )
    by_core = to_messages(column_grad[:COLUMN]).reshape(N_Z, 2, 8, 128)
    grad_out[0] = by_core[:, 0]
    grad_out[1] = by_core[:, 1]

    grad_over = core_copy(grad_out.at[1 - core], grad_core, 2)
    grad_over.start()
    item_grad_ref[...] = (dfeatures[:, E : 2 * E] + dfeatures[:, 2 * E :] * user_rows).astype(BF16)
    grad_over.wait_recv()
    grad_pair[...] = grad_out[core] + grad_core[...]

    def send_grad(s, _):
        step = alternate(s, N_Z)
        z_copy(grad_pair.at[wrap(z + step, N_Z)], grad_in.at[z], grad_send, grad_recv, step).start()
        return 0

    def wait_grad(s, _):
        arrived(grad_in, grad_recv, wrap(z + s, N_Z))
        return 0

    lax.fori_loop(1, N_Z, send_grad, 0)
    grad_in[z] = grad_pair[z]
    lax.fori_loop(8, N_Z, count_own_core, 0)
    ids_over.wait_recv()
    lax.fori_loop(0, 6, count_other_core, 0)
    lax.fori_loop(1, N_Z, wait_grad, 0)
    request_grad = jnp.sum(grad_in[...], axis=0)
    request_out[...] = request_grad
    request_in[y] = request_grad

    def y_copy(s):
        return pltpu.make_async_remote_copy(
            src_ref=request_out,
            dst_ref=request_in.at[y],
            send_sem=request_send.at[s],
            recv_sem=request_recv.at[y],
            device_id=(i, (k + s * N_X) % N_ROW),
            device_id_type=MESH,
        )

    for s in range(1, N_Y):
        y_copy(s).start()
    lax.fori_loop(6, 9, count_other_core, 0)
    for s in range(1, N_Y):
        arrived(request_in, request_recv, (y + s) % N_Y)
    left, right = from_messages(request_in[...])
    own_rows = pl.ds(pl.multiple_of(x * QUARTER, QUARTER), QUARTER)
    all_grads[core, z, own_rows, :128] = left.astype(BF16)
    all_grads[core, z, own_rows, 128:] = right.astype(BF16)

    def quarter(where, which):
        return all_grads.at[core, where, pl.ds(pl.multiple_of(which * QUARTER, QUARTER), QUARTER)]

    def send_z(s, _):
        z_copy(quarter(z, x), quarter(z, x), z_send, z_recv, alternate(s, N_Z)).start()
        return 0

    def x_copy(where, which, s):
        return pltpu.make_async_remote_copy(
            src_ref=quarter(where, which),
            dst_ref=quarter(where, which),
            send_sem=x_send.at[where, s],
            recv_sem=x_recv.at[where, which],
            device_id=(i, y * N_X + (x + s) % N_X),
            device_id_type=MESH,
        )

    def grads_over(where, side):
        return core_copy(all_grads.at[side, where], all_grads.at[side, where], 3 + where)

    lax.fori_loop(1, N_Z, send_z, 0)
    for step in range(1, N_X):
        x_copy(z, x, step).start()
    lax.fori_loop(9, N_Z, count_other_core, 0)

    def pass_on(s, _):
        where = wrap(z + alternate(s, N_Z), N_Z)
        block = quarter(where, x)
        pltpu.make_async_copy(block, block, z_recv.at[where]).wait()
        for step in range(1, N_X):
            x_copy(where, x, step).start()
        return 0

    lax.fori_loop(1, N_Z, pass_on, 0)

    def to_other_core(s, _):
        where = wrap(z + alternate(s, N_Z), N_Z)
        for step in range(1, N_X):
            which = (x + step) % N_X
            block = quarter(where, which)
            pltpu.make_async_copy(block, block, x_recv.at[where, which]).wait()
        grads_over(where, core).start()
        return 0

    lax.fori_loop(0, N_Z, to_other_core, 0)

    def product(side):
        columns = pl.ds(pl.multiple_of(side * (N_Z * GROUP), N_Z * GROUP), N_Z * GROUP)
        rows = all_grads[side].reshape(N_Z * GROUP, E)
        return jnp.dot(own_counts[:, columns], rows, preferred_element_type=F32)

    own_side = product(core)

    def wait_core(where, _):
        grads_over(where, 1 - core).wait_recv()
        return 0

    lax.fori_loop(0, N_Z, wait_core, 0)
    table_grad_ref[...] = own_side + product(1 - core)

    def drain_row(s, _):
        row_copy(partial_out.at[0], partial_in.at[k], partial_send, partial_recv, s).wait_send()
        return 0

    def drain_z(s, _):
        z_copy(ids_all.at[core, z], ids_all.at[core, z], ids_send, ids_recv, s).wait_send()
        z_copy(pooled_out, pooled_in.at[core, z], pooled_send, pooled_recv, s).wait_send()
        z_copy(grad_pair.at[0], grad_in.at[z], grad_send, grad_recv, s).wait_send()
        z_copy(quarter(z, x), quarter(z, x), z_send, z_recv, s).wait_send()
        return 0

    def drain_x(where, _):
        for step in range(1, N_X):
            x_copy(where, x, step).wait_send()
        grads_over(where, core).wait_send()
        return 0

    for s in range(1, N_Y):
        y_copy(s).wait_send()
    lax.fori_loop(1, N_ROW, drain_row, 0)
    lax.fori_loop(1, N_Z, drain_z, 0)
    lax.fori_loop(0, N_Z, drain_x, 0)
    ids_over.wait_send()
    pooled_over.wait_send()
    grad_over.wait_send()


def hand_over(table_grad_hbm, item_grad_hbm, table_grad_out, item_grad_out, table_grad, item_grad, sem):
    parts = []
    for n, (source, held, target) in enumerate(
        [(table_grad_hbm, table_grad, table_grad_out), (item_grad_hbm, item_grad, item_grad_out)]
    ):
        for part in range(2):
            rows = pl.ds(part * 128, 128)
            parts.append(
                (
                    pltpu.make_async_copy(source.at[rows], held.at[rows], sem.at[0, n, part]),
                    pltpu.make_async_copy(held.at[rows], target.at[rows], sem.at[1, n, part]),
                )
            )
    for load, _ in parts:
        load.start()
    for load, store in parts:
        load.wait()
        store.start()
    for _, store in parts:
        store.wait()


def per_device(user_table, user_ids, item_features, counts, placement, labels, w_hidden, bias, w_out):
    vmem = pl.BlockSpec(memory_space=pltpu.VMEM)
    hbm = pl.BlockSpec(memory_space=pl.ANY)
    dma = pltpu.SemaphoreType.DMA
    outs = (jax.ShapeDtypeStruct((SHARE, E), F32), jax.ShapeDtypeStruct((CAND, E), BF16))
    grads = pl.pallas_call(
        kernel,
        out_shape=outs,
        in_specs=[hbm] * 8 + [vmem],
        out_specs=(vmem, vmem),
        scratch_shapes=[
            pltpu.VMEM((ROWS, E), BF16),
            pltpu.VMEM((3 * E, H), BF16),
            pltpu.VMEM((BAG, GROUP), jnp.int32),
            pltpu.VMEM((CAND, E), BF16),
            pltpu.VMEM((1, COLUMN), jnp.int32),
            pltpu.VMEM((1, COLUMN), jnp.int32),
            pltpu.VMEM((1, CAND), jnp.int32),
            pltpu.VMEM((1, H), F32),
            pltpu.VMEM((GROUP, ROWS), BF16),
            pltpu.VMEM((N_ROW, 8, 128), F32),
            pltpu.VMEM((N_ROW, 8, 128), F32),
            pltpu.VMEM((8, 128), F32),
            pltpu.VMEM((2, N_Z, 8, 128), F32),
            pltpu.VMEM((128, E), BF16),
            pltpu.VMEM((2, N_Z, 8, 128), F32),
            pltpu.VMEM((N_Z, 8, 128), F32),
            pltpu.VMEM((N_Z, 8, 128), F32),
            pltpu.VMEM((N_Z, 8, 128), F32),
            pltpu.VMEM((8, 128), F32),
            pltpu.VMEM((N_Y, 8, 128), F32),
            pltpu.VMEM((2, N_Z, BAG, GROUP), jnp.int16),
            pltpu.VMEM((SHARE, N_DP * GROUP), BF16),
            pltpu.VMEM((2, N_Z, GROUP, E), BF16),
            dma((8,)),
            dma((N_Z,)),
            dma((N_Z,)),
            dma((N_ROW,)),
            dma((N_ROW,)),
            dma((N_Z,)),
            dma((N_Z,)),
            dma((N_Z,)),
            dma((N_Z,)),
            dma((N_Y,)),
            dma((N_Y,)),
            dma((N_Z,)),
            dma((N_Z,)),
            dma((N_Z, N_X)),
            dma((N_Z, N_X)),
            dma((3 + N_Z,)),
            dma((3 + N_Z,)),
        ],
        compiler_params=pltpu.CompilerParams(
            collective_id=0, has_side_effects=True, vmem_limit_bytes=60 * 1024 * 1024
        ),
    )(
        user_table,
        user_ids.T,
        item_features,
        counts,
        placement,
        labels.reshape(1, CAND),
        w_hidden,
        bias.reshape(1, H),
        w_out,
    )
    return pl.pallas_call(
        hand_over,
        out_shape=outs,
        in_specs=[hbm] * 2,
        out_specs=(hbm, hbm),
        scratch_shapes=[pltpu.VMEM((SHARE, E), F32), pltpu.VMEM((CAND, E), BF16), dma((2, 2, 2))],
        compiler_params=pltpu.CompilerParams(vmem_limit_bytes=60 * 1024 * 1024),
    )(*grads)


def solution(mesh):
    return jax.shard_map(
        per_device,
        mesh=mesh,
        in_specs=(
            P("row", None),
            P("dp", None),
            P(("dp", "row"), None),
            P("row", None),
            P("row", None),
            P(("dp", "row")),
            P(),
            P(),
            P(),
        ),
        out_specs=(P(("row", "dp"), None), P(("dp", "row"), None)),
        check_vma=False,
    )
```

```python
import functools

import jax
import jax.numpy as jnp
from jax import lax
from jax.experimental import pallas as pl
from jax.experimental.pallas import tpu as pltpu
from jax.sharding import PartitionSpec as P

MESH = pl.DeviceIdType.MESH
loss_scale = 64.0

N_DP = 24
N_ROW = 32
N_X = 4
N_Z = 12
REQ = 4
GROUP = N_ROW * REQ
COLUMN = N_DP * REQ
BAG = 32
E = 256
H = 1024
ROWS = 6144
SHARE = ROWS // N_DP
CAND = 256
QUARTER = GROUP // N_X
N_Y = N_ROW // N_X
BLOCK = 16
N_BLOCK = GROUP // BLOCK
BF16 = jnp.bfloat16
F32 = jnp.float32


def iota(shape, dim, dtype=jnp.int32):
    return lax.broadcasted_iota(jnp.int32, shape, dim).astype(dtype)


def to_messages(rows):
    n = rows.shape[0] // 8
    left = rows[:, :128].reshape(n, 8, 128)
    right = rows[:, 128:].reshape(n, 8, 128)
    upper = iota((n, 8, 128), 1) < 4
    even = jnp.where(upper, left, pltpu.roll(right, 4, axis=1))
    odd = jnp.where(upper, pltpu.roll(left, 4, axis=1), right)
    return jnp.stack([even, odd], axis=1).reshape(2 * n, 8, 128)


def from_messages(messages):
    n = messages.shape[0] // 2
    pairs = messages.reshape(n, 2, 8, 128)
    even, odd = pairs[:, 0], pairs[:, 1]
    upper = iota((n, 8, 128), 1) < 4
    left = jnp.where(upper, even, pltpu.roll(odd, 4, axis=1))
    right = jnp.where(upper, pltpu.roll(even, 4, axis=1), odd)
    return left.reshape(8 * n, 128), right.reshape(8 * n, 128)


def wrap(value, size):
    return jnp.where(value >= size, value - size, value)


def alternate(s, size):
    half = (s + 1) // 2
    return jnp.where(s % 2 == 1, half, wrap(size - half, size))


def flatten(turned):
    lag = (iota((8, 128), 0) + 8 - iota((8, 128), 1) // BLOCK) % 8
    parts = []
    for first in range(0, BAG, 8):
        tile = turned[first : first + 8]
        part = tile
        for d in range(1, 8):
            moved = pltpu.roll(pltpu.roll(tile, d, axis=0), 128 - BLOCK * d, axis=1)
            part = jnp.where(lag == d, moved, part)
        parts.append(part)
    return jnp.concatenate(parts, axis=1)


def kernel(
    table_hbm,
    ids_hbm,
    item_hbm,
    counts_hbm,
    placement_hbm,
    labels_hbm,
    w_hidden_hbm,
    bias_hbm,
    w_out_ref,
    table_grad_ref,
    item_grad_ref,
    table,
    w_hidden,
    ids_ref,
    item_ref,
    counts_ref,
    placement_ref,
    labels_ref,
    bias_ref,
    group_counts,
    partial_out,
    partial_in,
    pooled_out,
    pooled_in,
    pooled_column,
    grad_out,
    grad_core,
    grad_pair,
    grad_in,
    request_out,
    request_in,
    ids_all,
    own_counts,
    all_grads,
    load_sem,
    ids_send,
    ids_recv,
    partial_send,
    partial_recv,
    pooled_send,
    pooled_recv,
    grad_send,
    grad_recv,
    request_send,
    request_recv,
    z_send,
    z_recv,
    x_send,
    x_recv,
    core_send,
    core_recv,
):
    i = lax.axis_index("dp")
    k = lax.axis_index("row")
    z = i // 2
    core = i % 2
    y = k // N_X
    x = k % N_X

    ids_load = pltpu.make_async_copy(ids_hbm, ids_ref, load_sem.at[0])
    table_load = pltpu.make_async_copy(table_hbm, table, load_sem.at[1])
    later_loads = [
        pltpu.make_async_copy(source, target, load_sem.at[n])
        for n, (source, target) in enumerate(
            [
                (placement_hbm, placement_ref),
                (counts_hbm, counts_ref),
                (labels_hbm, labels_ref),
                (item_hbm, item_ref),
                (bias_hbm, bias_ref),
                (w_hidden_hbm, w_hidden),
            ],
            2,
        )
    ]
    ids_load.start()
    table_load.start()
    for load in later_loads:
        load.start()

    barrier = pltpu.get_barrier_semaphore()

    def greet_row(s, _):
        pl.semaphore_signal(barrier, inc=1, device_id=(i, (k + s) % N_ROW), device_id_type=MESH)
        return 0

    def greet_z(s, _):
        there = wrap(z + s, N_Z) * 2 + core
        pl.semaphore_signal(barrier, inc=1, device_id=(there, k), device_id_type=MESH)
        return 0

    lax.fori_loop(1, N_ROW, greet_row, 0)
    lax.fori_loop(1, N_Z, greet_z, 0)
    pl.semaphore_signal(barrier, inc=1, device_id=(z * 2 + 1 - core, k), device_id_type=MESH)

    ids_load.wait()
    relative = ids_ref[...] - k * ROWS
    relative = jnp.where((relative >= 0) & (relative < ROWS), relative, -1)
    flat = flatten(relative)
    in_block = iota((N_BLOCK, BLOCK * BAG), 1) % BLOCK
    high_key = jnp.where(flat >= 0, (flat >> 8) * BLOCK + in_block, -1)
    low_key = flat & (SHARE - 1)
    high_row = iota((N_DP * BLOCK, 1), 0)
    low_row = iota((SHARE, 1), 0)
    for b in range(N_BLOCK):
        high = jnp.where(high_key[b : b + 1] == high_row, 1.0, 0.0).astype(BF16)
        low = jnp.where(low_key[b : b + 1] == low_row, 1.0, 0.0).astype(BF16)
        found = lax.dot_general(high, low, (((1,), (1,)), ((), ())), preferred_element_type=F32).astype(BF16)
        for h in range(N_DP):
            group_counts[b * BLOCK : (b + 1) * BLOCK, h * SHARE : (h + 1) * SHARE] = found[
                h * BLOCK : (h + 1) * BLOCK
            ]
    table_load.wait()
    partial = jnp.dot(group_counts[...], table[...], preferred_element_type=F32)
    partial_out[...] = to_messages(partial)

    pl.semaphore_wait(barrier, N_ROW - 1 + N_Z)

    def row_copy(src, dst, send, recv, s):
        return pltpu.make_async_remote_copy(
            src_ref=src,
            dst_ref=dst,
            send_sem=send.at[s],
            recv_sem=recv.at[k],
            device_id=(i, (k + s) % N_ROW),
            device_id_type=MESH,
        )

    def z_copy(src, dst, send, recv, s):
        return pltpu.make_async_remote_copy(
            src_ref=src,
            dst_ref=dst,
            send_sem=send.at[s],
            recv_sem=recv.at[z],
            device_id=(wrap(z + s, N_Z) * 2 + core, k),
            device_id_type=MESH,
        )

    def core_copy(src, dst, n):
        return pltpu.make_async_remote_copy(
            src_ref=src,
            dst_ref=dst,
            send_sem=core_send.at[n],
            recv_sem=core_recv.at[n],
            device_id=(z * 2 + 1 - core, k),
            device_id_type=MESH,
        )

    def arrived(buffer, recv, source):
        pltpu.make_async_copy(buffer.at[source], buffer.at[source], recv.at[source]).wait()

    def send_partial(s, _):
        row_copy(partial_out.at[(k + s) % N_ROW], partial_in.at[k], partial_send, partial_recv, s).start()
        return 0

    lax.fori_loop(1, N_ROW, send_partial, 0)
    partial_in[k] = partial_out[k]

    to = iota((GROUP, GROUP), 1)
    moved_from = (to % QUARTER // REQ) * (N_X * REQ) + to // QUARTER * REQ + to % REQ
    reorder = jnp.where(iota((GROUP, GROUP), 0) == moved_from, 1.0, 0.0).astype(BF16)
    high_digit = (relative >> 8).astype(F32).astype(BF16)
    low_digit = (relative & (SHARE - 1)).astype(F32).astype(BF16)
    ids_moved = jnp.dot(high_digit, reorder, preferred_element_type=F32) * SHARE + jnp.dot(
        low_digit, reorder, preferred_element_type=F32
    )
    ids_all[core, z] = ids_moved.astype(jnp.int32).astype(jnp.int16)

    def send_ids(s, _):
        z_copy(ids_all.at[core, z], ids_all.at[core, z], ids_send, ids_recv, alternate(s, N_Z)).start()
        return 0

    lax.fori_loop(1, N_Z, send_ids, 0)

    own_first = i * SHARE

    def count_group(side, where):
        ids = jnp.clip(ids_all[side, where].astype(jnp.int32) - own_first, -1, SHARE).astype(F32)
        row = iota((SHARE, GROUP), 0, F32).astype(BF16)
        total = jnp.zeros((SHARE, GROUP), BF16)
        one, zero = jnp.ones((), BF16), jnp.zeros((), BF16)
        for b in range(BAG):
            wanted = jnp.broadcast_to(ids[b : b + 1], (16, GROUP)).astype(BF16)
            total = total + jnp.where(jnp.tile(wanted, (SHARE // 16, 1)) == row, one, zero)
        columns = pl.ds(pl.multiple_of((side * N_Z + where) * GROUP, GROUP), GROUP)
        own_counts[:, columns] = total

    def count_own_core(s, _):
        count_group(core, wrap(z + alternate(s, N_Z), N_Z))
        return 0

    def count_other_core(where, _):
        count_group(1 - core, where)
        return 0

    for load in later_loads:
        load.wait()
    padding = jnp.zeros((1, 128 - COLUMN), jnp.int32)
    order = jnp.concatenate([placement_ref[...], padding - 1], axis=1)
    column_counts = jnp.concatenate([counts_ref[...], padding], axis=1).astype(F32)
    eye = iota((128, 128), 0) == iota((128, 128), 1)
    place_at = jnp.where(order == iota((128, 128), 0), iota((128, 128), 1).astype(F32), 0.0)
    position = jnp.sum(place_at, axis=1, keepdims=True)
    position_row = jnp.sum(jnp.where(eye, position, 0.0), axis=0, keepdims=True)
    start = jnp.sum(jnp.where(position_row < position, column_counts, 0.0), axis=1, keepdims=True)
    count = jnp.sum(jnp.where(eye, column_counts, 0.0), axis=1, keepdims=True)
    start_row = jnp.sum(jnp.where(eye, start, 0.0), axis=0, keepdims=True)
    end, end_row = start + count, start_row + column_counts
    first = (i * CAND).astype(F32)
    slot = first + iota((CAND, 1), 0, F32)
    slot_row = first + iota((1, CAND), 1, F32)
    member = jnp.where((slot >= start_row) & (slot < end_row), 1.0, 0.0).astype(BF16)
    member_turned = jnp.where((slot_row >= start) & (slot_row < end), 1.0, 0.0).astype(BF16)
    diagonal = iota((CAND, CAND), 0) == iota((CAND, CAND), 1)
    label = jnp.sum(jnp.where(diagonal, labels_ref[...].astype(F32), 0.0), axis=1, keepdims=True)

    item = item_ref[...]
    item_wide = item.astype(F32)
    item_pre = jnp.dot(item, w_hidden[E : 2 * E], preferred_element_type=F32) + bias_ref[...]

    count_group(core, z)

    def wait_partial(s, _):
        arrived(partial_in, partial_recv, (k + s) % N_ROW)
        return 0

    lax.fori_loop(1, N_ROW, wait_partial, 0)
    pooled = jnp.sum(partial_in[...], axis=0)
    pooled_out[...] = pooled
    pooled_in[core, z] = pooled

    def send_pooled(s, _):
        z_copy(pooled_out, pooled_in.at[core, z], pooled_send, pooled_recv, alternate(s, N_Z)).start()
        return 0

    def wait_ids(s, _):
        where = wrap(z + s, N_Z)
        block = ids_all.at[core, where]
        pltpu.make_async_copy(block, block, ids_recv.at[where]).wait()
        return 0

    def wait_pooled(s, _):
        where = wrap(z + s, N_Z)
        block = pooled_in.at[core, where]
        pltpu.make_async_copy(block, block, pooled_recv.at[where]).wait()
        return 0

    lax.fori_loop(1, N_Z, send_pooled, 0)
    pooled_column[...] = jnp.zeros_like(pooled_column)
    lax.fori_loop(1, N_Z, wait_ids, 0)
    lax.fori_loop(1, 8, count_own_core, 0)
    lax.fori_loop(1, N_Z, wait_pooled, 0)
    pooled_over = core_copy(pooled_in.at[core], pooled_in.at[core], 1)
    pooled_over.start()
    ids_over = core_copy(ids_all.at[core], ids_all.at[core], 0)
    ids_over.start()
    pooled_over.wait_recv()
    pooled_all = jnp.stack([pooled_in[0], pooled_in[1]], axis=1).reshape(N_DP, 8, 128)
    left, right = from_messages(pooled_all)
    pooled_column[:COLUMN, :128] = left.astype(BF16)
    pooled_column[:COLUMN, 128:] = right.astype(BF16)

    user_rows = jnp.dot(member, pooled_column[...], preferred_element_type=F32)
    user = user_rows.astype(BF16)
    both = (user_rows * item_wide).astype(BF16)
    pre = (
        item_pre
        + jnp.dot(user, w_hidden[:E], preferred_element_type=F32)
        + jnp.dot(both, w_hidden[2 * E :], preferred_element_type=F32)
    )
    sigma = jax.nn.sigmoid(pre)
    hidden = (pre * sigma).astype(BF16).astype(F32)
    w_out = w_out_ref[...].astype(F32).reshape(1, H)
    score = jnp.sum(hidden * w_out, axis=1, keepdims=True)
    dscore = loss_scale * (jax.nn.sigmoid(score) - label)
    slope = sigma * (1.0 + pre * (1.0 - sigma))
    dhidden = (dscore * w_out * slope).astype(BF16)
    dfeatures = lax.dot_general(dhidden, w_hidden[...], (((1,), (1,)), ((), ())), preferred_element_type=F32)
    user_grad = dfeatures[:, :E] + dfeatures[:, 2 * E :] * item_wide
    coarse = user_grad.astype(BF16)
    fine = (user_grad - coarse.astype(F32)).astype(BF16)
    column_grad = jnp.dot(member_turned, coarse, preferred_element_type=F32) + jnp.dot(
        member_turned, fine, preferred_element_type=F32
    )
    by_core = to_messages(column_grad[:COLUMN]).reshape(N_Z, 2, 8, 128)
    grad_out[0] = by_core[:, 0]
    grad_out[1] = by_core[:, 1]

    grad_over = core_copy(grad_out.at[1 - core], grad_core, 2)
    grad_over.start()
    item_grad_ref[...] = (dfeatures[:, E : 2 * E] + dfeatures[:, 2 * E :] * user_rows).astype(BF16)
    grad_over.wait_recv()
    grad_pair[...] = grad_out[core] + grad_core[...]

    def send_grad(s, _):
        step = alternate(s, N_Z)
        z_copy(grad_pair.at[wrap(z + step, N_Z)], grad_in.at[z], grad_send, grad_recv, step).start()
        return 0

    def wait_grad(s, _):
        arrived(grad_in, grad_recv, wrap(z + s, N_Z))
        return 0

    lax.fori_loop(1, N_Z, send_grad, 0)
    grad_in[z] = grad_pair[z]
    lax.fori_loop(8, N_Z, count_own_core, 0)
    ids_over.wait_recv()
    lax.fori_loop(0, 6, count_other_core, 0)
    lax.fori_loop(1, N_Z, wait_grad, 0)
    request_grad = jnp.sum(grad_in[...], axis=0)
    request_out[...] = request_grad
    request_in[y] = request_grad

    def y_copy(s):
        return pltpu.make_async_remote_copy(
            src_ref=request_out,
            dst_ref=request_in.at[y],
            send_sem=request_send.at[s],
            recv_sem=request_recv.at[y],
            device_id=(i, (k + s * N_X) % N_ROW),
            device_id_type=MESH,
        )

    for s in range(1, N_Y):
        y_copy(s).start()
    lax.fori_loop(6, 9, count_other_core, 0)
    for s in range(1, N_Y):
        arrived(request_in, request_recv, (y + s) % N_Y)
    left, right = from_messages(request_in[...])
    own_rows = pl.ds(pl.multiple_of(x * QUARTER, QUARTER), QUARTER)
    all_grads[core, z, own_rows, :128] = left.astype(BF16)
    all_grads[core, z, own_rows, 128:] = right.astype(BF16)

    def quarter(where, which):
        return all_grads.at[core, where, pl.ds(pl.multiple_of(which * QUARTER, QUARTER), QUARTER)]

    def send_z(s, _):
        z_copy(quarter(z, x), quarter(z, x), z_send, z_recv, alternate(N_Z - s, N_Z)).start()
        return 0

    def half(where, which, part):
        first = pl.multiple_of(which * QUARTER + part * (QUARTER // 2), QUARTER // 2)
        return all_grads.at[core, where, pl.ds(first, QUARTER // 2)]

    def x_copy(where, step):
        side = (1 - step) // 2
        return pltpu.make_async_remote_copy(
            src_ref=quarter(where, x),
            dst_ref=quarter(where, x),
            send_sem=x_send.at[where, side],
            recv_sem=x_recv.at[where, side],
            device_id=(i, y * N_X + (x + step + N_X) % N_X),
            device_id_type=MESH,
        )

    def x_wait(where, step):
        side = (1 - step) // 2
        block = quarter(where, (x - step + N_X) % N_X)
        pltpu.make_async_copy(block, block, x_recv.at[where, side]).wait()

    def x_pass(where, step):
        side = (1 - step) // 2
        block = half(where, (x - step + N_X) % N_X, side)
        return pltpu.make_async_remote_copy(
            src_ref=block,
            dst_ref=block,
            send_sem=x_send.at[where, 2 + side],
            recv_sem=x_recv.at[where, 2 + side],
            device_id=(i, y * N_X + (x + step + N_X) % N_X),
            device_id_type=MESH,
        )

    def x_pass_wait(where, step):
        side = (1 - step) // 2
        block = half(where, (x + 2) % N_X, side)
        pltpu.make_async_copy(block, block, x_recv.at[where, 2 + side]).wait()

    def grads_over(where, side):
        return core_copy(all_grads.at[side, where], all_grads.at[side, where], 3 + where)

    def at_step(s):
        return wrap(z + alternate(s, N_Z), N_Z)

    def pass_on(where):
        for step in (1, -1):
            x_wait(where, step)
            x_pass(where, step).start()

    def to_other_core(where):
        for step in (1, -1):
            x_pass_wait(where, step)
        grads_over(where, core).start()

    lax.fori_loop(1, N_Z, send_z, 0)
    for step in (1, -1):
        x_copy(z, step).start()
    lax.fori_loop(9, N_Z, count_other_core, 0)

    def advance(s, _):
        where = at_step(s)
        block = quarter(where, x)
        pltpu.make_async_copy(block, block, z_recv.at[where]).wait()
        for step in (1, -1):
            x_copy(where, step).start()
        pass_on(at_step(s - 1))

        @pl.when(s >= 2)
        def _():
            to_other_core(at_step(s - 2))

        return 0

    lax.fori_loop(1, N_Z, advance, 0)
    pass_on(at_step(N_Z - 1))
    to_other_core(at_step(N_Z - 2))
    to_other_core(at_step(N_Z - 1))

    def product(side):
        columns = pl.ds(pl.multiple_of(side * (N_Z * GROUP), N_Z * GROUP), N_Z * GROUP)
        rows = all_grads[side].reshape(N_Z * GROUP, E)
        return jnp.dot(own_counts[:, columns], rows, preferred_element_type=F32)

    own_side = product(core)

    def wait_core(where, _):
        grads_over(where, 1 - core).wait_recv()
        return 0

    lax.fori_loop(0, N_Z, wait_core, 0)
    table_grad_ref[...] = own_side + product(1 - core)

    def drain_row(s, _):
        row_copy(partial_out.at[0], partial_in.at[k], partial_send, partial_recv, s).wait_send()
        return 0

    def drain_z(s, _):
        z_copy(ids_all.at[core, z], ids_all.at[core, z], ids_send, ids_recv, s).wait_send()
        z_copy(pooled_out, pooled_in.at[core, z], pooled_send, pooled_recv, s).wait_send()
        z_copy(grad_pair.at[0], grad_in.at[z], grad_send, grad_recv, s).wait_send()
        z_copy(quarter(z, x), quarter(z, x), z_send, z_recv, s).wait_send()
        return 0

    def drain_x(where, _):
        for step in (1, -1):
            x_copy(where, step).wait_send()
            x_pass(where, step).wait_send()
        grads_over(where, core).wait_send()
        return 0

    for s in range(1, N_Y):
        y_copy(s).wait_send()
    lax.fori_loop(1, N_ROW, drain_row, 0)
    lax.fori_loop(1, N_Z, drain_z, 0)
    lax.fori_loop(0, N_Z, drain_x, 0)
    ids_over.wait_send()
    pooled_over.wait_send()
    grad_over.wait_send()


def hand_over(table_grad_hbm, item_grad_hbm, table_grad_out, item_grad_out, table_grad, item_grad, sem):
    parts = []
    for n, (source, held, target) in enumerate(
        [(table_grad_hbm, table_grad, table_grad_out), (item_grad_hbm, item_grad, item_grad_out)]
    ):
        for part in range(2):
            rows = pl.ds(part * 128, 128)
            parts.append(
                (
                    pltpu.make_async_copy(source.at[rows], held.at[rows], sem.at[0, n, part]),
                    pltpu.make_async_copy(held.at[rows], target.at[rows], sem.at[1, n, part]),
                )
            )
    for load, _ in parts:
        load.start()
    for load, store in parts:
        load.wait()
        store.start()
    for _, store in parts:
        store.wait()


def per_device(user_table, user_ids, item_features, counts, placement, labels, w_hidden, bias, w_out):
    vmem = pl.BlockSpec(memory_space=pltpu.VMEM)
    hbm = pl.BlockSpec(memory_space=pl.ANY)
    dma = pltpu.SemaphoreType.DMA
    outs = (jax.ShapeDtypeStruct((SHARE, E), F32), jax.ShapeDtypeStruct((CAND, E), BF16))
    grads = pl.pallas_call(
        kernel,
        out_shape=outs,
        in_specs=[hbm] * 8 + [vmem],
        out_specs=(vmem, vmem),
        scratch_shapes=[
            pltpu.VMEM((ROWS, E), BF16),
            pltpu.VMEM((3 * E, H), BF16),
            pltpu.VMEM((BAG, GROUP), jnp.int32),
            pltpu.VMEM((CAND, E), BF16),
            pltpu.VMEM((1, COLUMN), jnp.int32),
            pltpu.VMEM((1, COLUMN), jnp.int32),
            pltpu.VMEM((1, CAND), jnp.int32),
            pltpu.VMEM((1, H), F32),
            pltpu.VMEM((GROUP, ROWS), BF16),
            pltpu.VMEM((N_ROW, 8, 128), F32),
            pltpu.VMEM((N_ROW, 8, 128), F32),
            pltpu.VMEM((8, 128), F32),
            pltpu.VMEM((2, N_Z, 8, 128), F32),
            pltpu.VMEM((128, E), BF16),
            pltpu.VMEM((2, N_Z, 8, 128), F32),
            pltpu.VMEM((N_Z, 8, 128), F32),
            pltpu.VMEM((N_Z, 8, 128), F32),
            pltpu.VMEM((N_Z, 8, 128), F32),
            pltpu.VMEM((8, 128), F32),
            pltpu.VMEM((N_Y, 8, 128), F32),
            pltpu.VMEM((2, N_Z, BAG, GROUP), jnp.int16),
            pltpu.VMEM((SHARE, N_DP * GROUP), BF16),
            pltpu.VMEM((2, N_Z, GROUP, E), BF16),
            dma((8,)),
            dma((N_Z,)),
            dma((N_Z,)),
            dma((N_ROW,)),
            dma((N_ROW,)),
            dma((N_Z,)),
            dma((N_Z,)),
            dma((N_Z,)),
            dma((N_Z,)),
            dma((N_Y,)),
            dma((N_Y,)),
            dma((N_Z,)),
            dma((N_Z,)),
            dma((N_Z, N_X)),
            dma((N_Z, N_X)),
            dma((3 + N_Z,)),
            dma((3 + N_Z,)),
        ],
        compiler_params=pltpu.CompilerParams(
            collective_id=0, has_side_effects=True, vmem_limit_bytes=60 * 1024 * 1024
        ),
    )(
        user_table,
        user_ids.T,
        item_features,
        counts,
        placement,
        labels.reshape(1, CAND),
        w_hidden,
        bias.reshape(1, H),
        w_out,
    )
    return pl.pallas_call(
        hand_over,
        out_shape=outs,
        in_specs=[hbm] * 2,
        out_specs=(hbm, hbm),
        scratch_shapes=[pltpu.VMEM((SHARE, E), F32), pltpu.VMEM((CAND, E), BF16), dma((2, 2, 2))],
        compiler_params=pltpu.CompilerParams(vmem_limit_bytes=60 * 1024 * 1024),
    )(*grads)


def solution(mesh):
    return jax.shard_map(
        per_device,
        mesh=mesh,
        in_specs=(
            P("row", None),
            P("dp", None),
            P(("dp", "row"), None),
            P("row", None),
            P("row", None),
            P(("dp", "row")),
            P(),
            P(),
            P(),
        ),
        out_specs=(P(("row", "dp"), None), P(("dp", "row"), None)),
        check_vma=False,
    )
```

```python
import functools

import jax
import jax.numpy as jnp
from jax import lax
from jax.experimental import pallas as pl
from jax.experimental.pallas import tpu as pltpu
from jax.sharding import PartitionSpec as P

MESH = pl.DeviceIdType.MESH
loss_scale = 64.0

N_DP = 24
N_ROW = 32
N_X = 4
N_Z = 12
REQ = 4
GROUP = N_ROW * REQ
COLUMN = N_DP * REQ
BAG = 32
E = 256
H = 1024
ROWS = 6144
SHARE = ROWS // N_DP
CAND = 256
QUARTER = GROUP // N_X
N_Y = N_ROW // N_X
BLOCK = 16
N_BLOCK = GROUP // BLOCK
BF16 = jnp.bfloat16
F32 = jnp.float32


def iota(shape, dim, dtype=jnp.int32):
    return lax.broadcasted_iota(jnp.int32, shape, dim).astype(dtype)


ROW_STEPS = [(v, u) for v in (4, 3, 5, 2, 6, 1, 7, 0) for u in (2, 1, 3, 0) if (v, u) != (0, 0)]


def to_messages(rows):
    n = rows.shape[0] // 8
    left = rows[:, :128].reshape(n, 8, 128)
    right = rows[:, 128:].reshape(n, 8, 128)
    upper = iota((n, 8, 128), 1) < 4
    even = jnp.where(upper, left, pltpu.roll(right, 4, axis=1))
    odd = jnp.where(upper, pltpu.roll(left, 4, axis=1), right)
    return jnp.stack([even, odd], axis=1).reshape(2 * n, 8, 128)


def from_messages(messages):
    n = messages.shape[0] // 2
    pairs = messages.reshape(n, 2, 8, 128)
    even, odd = pairs[:, 0], pairs[:, 1]
    upper = iota((n, 8, 128), 1) < 4
    left = jnp.where(upper, even, pltpu.roll(odd, 4, axis=1))
    right = jnp.where(upper, pltpu.roll(even, 4, axis=1), odd)
    return left.reshape(8 * n, 128), right.reshape(8 * n, 128)


def wrap(value, size):
    return jnp.where(value >= size, value - size, value)


def alternate(s, size):
    half = (s + 1) // 2
    return jnp.where(s % 2 == 1, half, wrap(size - half, size))


def flatten(turned):
    lag = (iota((8, 128), 0) + 8 - iota((8, 128), 1) // BLOCK) % 8
    parts = []
    for first in range(0, BAG, 8):
        tile = turned[first : first + 8]
        part = tile
        for d in range(1, 8):
            moved = pltpu.roll(pltpu.roll(tile, d, axis=0), 128 - BLOCK * d, axis=1)
            part = jnp.where(lag == d, moved, part)
        parts.append(part)
    return jnp.concatenate(parts, axis=1)


def kernel(
    table_hbm,
    ids_hbm,
    item_hbm,
    counts_hbm,
    placement_hbm,
    labels_hbm,
    w_hidden_hbm,
    bias_hbm,
    w_out_ref,
    table_grad_ref,
    item_grad_ref,
    table,
    w_hidden,
    ids_ref,
    item_ref,
    counts_ref,
    placement_ref,
    labels_ref,
    bias_ref,
    group_counts,
    partial_out,
    partial_in,
    pooled_out,
    pooled_in,
    pooled_column,
    grad_out,
    grad_core,
    grad_pair,
    grad_in,
    request_out,
    request_in,
    ids_all,
    own_counts,
    all_grads,
    load_sem,
    ids_send,
    ids_recv,
    partial_send,
    partial_recv,
    pooled_send,
    pooled_recv,
    grad_send,
    grad_recv,
    request_send,
    request_recv,
    z_send,
    z_recv,
    x_send,
    x_recv,
    core_send,
    core_recv,
):
    i = lax.axis_index("dp")
    k = lax.axis_index("row")
    z = i // 2
    core = i % 2
    y = k // N_X
    x = k % N_X

    ids_load = pltpu.make_async_copy(ids_hbm, ids_ref, load_sem.at[0])
    table_load = pltpu.make_async_copy(table_hbm, table, load_sem.at[1])
    later_loads = [
        pltpu.make_async_copy(source, target, load_sem.at[n])
        for n, (source, target) in enumerate(
            [
                (placement_hbm, placement_ref),
                (counts_hbm, counts_ref),
                (labels_hbm, labels_ref),
                (item_hbm, item_ref),
                (bias_hbm, bias_ref),
                (w_hidden_hbm, w_hidden),
            ],
            2,
        )
    ]
    ids_load.start()
    table_load.start()
    for load in later_loads:
        load.start()

    barrier = pltpu.get_barrier_semaphore()

    def in_row(step):
        return (y + step[0]) % N_Y * N_X + (x + step[1]) % N_X

    def greet_z(s, _):
        there = wrap(z + alternate(N_Z - s, N_Z), N_Z) * 2 + core
        pl.semaphore_signal(barrier, inc=1, device_id=(there, k), device_id_type=MESH)
        return 0

    def greet_row(steps):
        for step in steps:
            pl.semaphore_signal(barrier, inc=1, device_id=(i, in_row(step)), device_id_type=MESH)

    greet_row(ROW_STEPS[:12])
    lax.fori_loop(1, N_Z, greet_z, 0)
    greet_row(ROW_STEPS[12:])
    pl.semaphore_signal(barrier, inc=1, device_id=(z * 2 + 1 - core, k), device_id_type=MESH)

    ids_load.wait()
    relative = ids_ref[...] - k * ROWS
    relative = jnp.where((relative >= 0) & (relative < ROWS), relative, -1)
    flat = flatten(relative)
    in_block = iota((N_BLOCK, BLOCK * BAG), 1) % BLOCK
    high_key = jnp.where(flat >= 0, (flat >> 8) * BLOCK + in_block, -1)
    low_key = flat & (SHARE - 1)
    high_row = iota((N_DP * BLOCK, 1), 0)
    low_row = iota((SHARE, 1), 0)
    for b in range(N_BLOCK):
        high = jnp.where(high_key[b : b + 1] == high_row, 1.0, 0.0).astype(BF16)
        low = jnp.where(low_key[b : b + 1] == low_row, 1.0, 0.0).astype(BF16)
        found = lax.dot_general(high, low, (((1,), (1,)), ((), ())), preferred_element_type=F32).astype(BF16)
        for h in range(N_DP):
            group_counts[b * BLOCK : (b + 1) * BLOCK, h * SHARE : (h + 1) * SHARE] = found[
                h * BLOCK : (h + 1) * BLOCK
            ]
    table_load.wait()
    partial = jnp.dot(group_counts[...], table[...], preferred_element_type=F32)
    partial_out[...] = to_messages(partial)

    pl.semaphore_wait(barrier, N_ROW - 1 + N_Z)

    def row_copy(src, dst, send, recv, step):
        return pltpu.make_async_remote_copy(
            src_ref=src,
            dst_ref=dst,
            send_sem=send.at[step[0] * N_X + step[1]],
            recv_sem=recv.at[k],
            device_id=(i, in_row(step)),
            device_id_type=MESH,
        )

    def z_copy(src, dst, send, recv, s):
        return pltpu.make_async_remote_copy(
            src_ref=src,
            dst_ref=dst,
            send_sem=send.at[s],
            recv_sem=recv.at[z],
            device_id=(wrap(z + s, N_Z) * 2 + core, k),
            device_id_type=MESH,
        )

    def core_copy(src, dst, n):
        return pltpu.make_async_remote_copy(
            src_ref=src,
            dst_ref=dst,
            send_sem=core_send.at[n],
            recv_sem=core_recv.at[n],
            device_id=(z * 2 + 1 - core, k),
            device_id_type=MESH,
        )

    def arrived(buffer, recv, source):
        pltpu.make_async_copy(buffer.at[source], buffer.at[source], recv.at[source]).wait()

    for step in ROW_STEPS:
        row_copy(partial_out.at[in_row(step)], partial_in.at[k], partial_send, partial_recv, step).start()
    partial_in[k] = partial_out[k]

    to = iota((GROUP, GROUP), 1)
    moved_from = (to % QUARTER // REQ) * (N_X * REQ) + to // QUARTER * REQ + to % REQ
    reorder = jnp.where(iota((GROUP, GROUP), 0) == moved_from, 1.0, 0.0).astype(BF16)
    high_digit = (relative >> 8).astype(F32).astype(BF16)
    low_digit = (relative & (SHARE - 1)).astype(F32).astype(BF16)
    ids_moved = jnp.dot(high_digit, reorder, preferred_element_type=F32) * SHARE + jnp.dot(
        low_digit, reorder, preferred_element_type=F32
    )
    ids_all[core, z] = ids_moved.astype(jnp.int32).astype(jnp.int16)

    def send_ids(s, _):
        z_copy(ids_all.at[core, z], ids_all.at[core, z], ids_send, ids_recv, alternate(s, N_Z)).start()
        return 0

    lax.fori_loop(1, N_Z, send_ids, 0)

    own_first = i * SHARE

    def count_group(side, where):
        ids = jnp.clip(ids_all[side, where].astype(jnp.int32) - own_first, -1, SHARE).astype(F32)
        row = iota((SHARE, GROUP), 0, F32).astype(BF16)
        total = jnp.zeros((SHARE, GROUP), BF16)
        one, zero = jnp.ones((), BF16), jnp.zeros((), BF16)
        for b in range(BAG):
            wanted = jnp.broadcast_to(ids[b : b + 1], (16, GROUP)).astype(BF16)
            total = total + jnp.where(jnp.tile(wanted, (SHARE // 16, 1)) == row, one, zero)
        columns = pl.ds(pl.multiple_of((side * N_Z + where) * GROUP, GROUP), GROUP)
        own_counts[:, columns] = total

    def count_own_core(s, _):
        count_group(core, wrap(z + alternate(s, N_Z), N_Z))
        return 0

    def count_other_core(where, _):
        count_group(1 - core, where)
        return 0

    for load in later_loads:
        load.wait()
    padding = jnp.zeros((1, 128 - COLUMN), jnp.int32)
    order = jnp.concatenate([placement_ref[...], padding - 1], axis=1)
    column_counts = jnp.concatenate([counts_ref[...], padding], axis=1).astype(F32)
    eye = iota((128, 128), 0) == iota((128, 128), 1)
    place_at = jnp.where(order == iota((128, 128), 0), iota((128, 128), 1).astype(F32), 0.0)
    position = jnp.sum(place_at, axis=1, keepdims=True)
    position_row = jnp.sum(jnp.where(eye, position, 0.0), axis=0, keepdims=True)
    start = jnp.sum(jnp.where(position_row < position, column_counts, 0.0), axis=1, keepdims=True)
    count = jnp.sum(jnp.where(eye, column_counts, 0.0), axis=1, keepdims=True)
    start_row = jnp.sum(jnp.where(eye, start, 0.0), axis=0, keepdims=True)
    end, end_row = start + count, start_row + column_counts
    first = (i * CAND).astype(F32)
    slot = first + iota((CAND, 1), 0, F32)
    slot_row = first + iota((1, CAND), 1, F32)
    member = jnp.where((slot >= start_row) & (slot < end_row), 1.0, 0.0).astype(BF16)
    member_turned = jnp.where((slot_row >= start) & (slot_row < end), 1.0, 0.0).astype(BF16)
    diagonal = iota((CAND, CAND), 0) == iota((CAND, CAND), 1)
    label = jnp.sum(jnp.where(diagonal, labels_ref[...].astype(F32), 0.0), axis=1, keepdims=True)

    item = item_ref[...]
    item_wide = item.astype(F32)
    item_pre = jnp.dot(item, w_hidden[E : 2 * E], preferred_element_type=F32) + bias_ref[...]

    count_group(core, z)

    def wait_partial(s, _):
        arrived(partial_in, partial_recv, (k + s) % N_ROW)
        return 0

    lax.fori_loop(1, N_ROW, wait_partial, 0)
    pooled = jnp.sum(partial_in[...], axis=0)
    pooled_out[...] = pooled
    pooled_in[core, z] = pooled

    def send_pooled(s, _):
        z_copy(pooled_out, pooled_in.at[core, z], pooled_send, pooled_recv, alternate(N_Z - s, N_Z)).start()
        return 0

    def wait_ids(s, _):
        where = wrap(z + s, N_Z)
        block = ids_all.at[core, where]
        pltpu.make_async_copy(block, block, ids_recv.at[where]).wait()
        return 0

    def wait_pooled(s, _):
        where = wrap(z + s, N_Z)
        block = pooled_in.at[core, where]
        pltpu.make_async_copy(block, block, pooled_recv.at[where]).wait()
        return 0

    lax.fori_loop(1, N_Z, send_pooled, 0)
    pooled_column[...] = jnp.zeros_like(pooled_column)
    lax.fori_loop(1, N_Z, wait_ids, 0)
    lax.fori_loop(1, 8, count_own_core, 0)
    lax.fori_loop(1, N_Z, wait_pooled, 0)
    pooled_over = core_copy(pooled_in.at[core], pooled_in.at[core], 1)
    pooled_over.start()
    ids_over = core_copy(ids_all.at[core], ids_all.at[core], 0)
    ids_over.start()
    pooled_over.wait_recv()
    pooled_all = jnp.stack([pooled_in[0], pooled_in[1]], axis=1).reshape(N_DP, 8, 128)
    left, right = from_messages(pooled_all)
    pooled_column[:COLUMN, :128] = left.astype(BF16)
    pooled_column[:COLUMN, 128:] = right.astype(BF16)

    user_rows = jnp.dot(member, pooled_column[...], preferred_element_type=F32)
    user = user_rows.astype(BF16)
    both = (user_rows * item_wide).astype(BF16)
    pre = (
        item_pre
        + jnp.dot(user, w_hidden[:E], preferred_element_type=F32)
        + jnp.dot(both, w_hidden[2 * E :], preferred_element_type=F32)
    )
    sigma = jax.nn.sigmoid(pre)
    hidden = (pre * sigma).astype(BF16).astype(F32)
    w_out = w_out_ref[...].astype(F32).reshape(1, H)
    score = jnp.sum(hidden * w_out, axis=1, keepdims=True)
    dscore = loss_scale * (jax.nn.sigmoid(score) - label)
    slope = sigma * (1.0 + pre * (1.0 - sigma))
    dhidden = (dscore * w_out * slope).astype(BF16)
    dfeatures = lax.dot_general(dhidden, w_hidden[...], (((1,), (1,)), ((), ())), preferred_element_type=F32)
    user_grad = dfeatures[:, :E] + dfeatures[:, 2 * E :] * item_wide
    coarse = user_grad.astype(BF16)
    fine = (user_grad - coarse.astype(F32)).astype(BF16)
    column_grad = jnp.dot(member_turned, coarse, preferred_element_type=F32) + jnp.dot(
        member_turned, fine, preferred_element_type=F32
    )
    by_core = to_messages(column_grad[:COLUMN]).reshape(N_Z, 2, 8, 128)
    grad_out[0] = by_core[:, 0]
    grad_out[1] = by_core[:, 1]

    grad_over = core_copy(grad_out.at[1 - core], grad_core, 2)
    grad_over.start()
    item_grad_ref[...] = (dfeatures[:, E : 2 * E] + dfeatures[:, 2 * E :] * user_rows).astype(BF16)
    grad_over.wait_recv()
    grad_pair[...] = grad_out[core] + grad_core[...]

    def send_grad(s, _):
        step = alternate(N_Z - s, N_Z)
        z_copy(grad_pair.at[wrap(z + step, N_Z)], grad_in.at[z], grad_send, grad_recv, step).start()
        return 0

    def wait_grad(s, _):
        arrived(grad_in, grad_recv, wrap(z + s, N_Z))
        return 0

    lax.fori_loop(1, N_Z, send_grad, 0)
    grad_in[z] = grad_pair[z]
    lax.fori_loop(8, N_Z, count_own_core, 0)
    ids_over.wait_recv()
    lax.fori_loop(0, 6, count_other_core, 0)
    lax.fori_loop(1, N_Z, wait_grad, 0)
    request_grad = jnp.sum(grad_in[...], axis=0)
    request_out[...] = request_grad
    request_in[y] = request_grad

    def y_copy(s):
        return pltpu.make_async_remote_copy(
            src_ref=request_out,
            dst_ref=request_in.at[y],
            send_sem=request_send.at[s],
            recv_sem=request_recv.at[y],
            device_id=(i, (k + s * N_X) % N_ROW),
            device_id_type=MESH,
        )

    for s in (4, 3, 5, 2, 6, 1, 7):
        y_copy(s).start()
    lax.fori_loop(6, 9, count_other_core, 0)
    for s in range(1, N_Y):
        arrived(request_in, request_recv, (y + s) % N_Y)
    left, right = from_messages(request_in[...])
    own_rows = pl.ds(pl.multiple_of(x * QUARTER, QUARTER), QUARTER)
    all_grads[core, z, own_rows, :128] = left.astype(BF16)
    all_grads[core, z, own_rows, 128:] = right.astype(BF16)

    def quarter(where, which):
        return all_grads.at[core, where, pl.ds(pl.multiple_of(which * QUARTER, QUARTER), QUARTER)]

    def send_z(s, _):
        z_copy(quarter(z, x), quarter(z, x), z_send, z_recv, alternate(s, N_Z)).start()
        return 0

    def x_copy(where, which, s):
        return pltpu.make_async_remote_copy(
            src_ref=quarter(where, which),
            dst_ref=quarter(where, which),
            send_sem=x_send.at[where, s],
            recv_sem=x_recv.at[where, which],
            device_id=(i, y * N_X + (x + s) % N_X),
            device_id_type=MESH,
        )

    def grads_over(where, side):
        return core_copy(all_grads.at[side, where], all_grads.at[side, where], 3 + where)

    lax.fori_loop(1, N_Z, send_z, 0)
    for step in range(1, N_X):
        x_copy(z, x, step).start()
    lax.fori_loop(9, N_Z, count_other_core, 0)

    def pass_on(s, _):
        where = wrap(z + alternate(s, N_Z), N_Z)
        block = quarter(where, x)
        pltpu.make_async_copy(block, block, z_recv.at[where]).wait()
        for step in range(1, N_X):
            x_copy(where, x, step).start()
        return 0

    lax.fori_loop(1, N_Z, pass_on, 0)

    def to_other_core(s, _):
        where = wrap(z + alternate(s, N_Z), N_Z)
        for step in range(1, N_X):
            which = (x + step) % N_X
            block = quarter(where, which)
            pltpu.make_async_copy(block, block, x_recv.at[where, which]).wait()
        grads_over(where, core).start()
        return 0

    lax.fori_loop(0, N_Z, to_other_core, 0)

    def product(side):
        columns = pl.ds(pl.multiple_of(side * (N_Z * GROUP), N_Z * GROUP), N_Z * GROUP)
        rows = all_grads[side].reshape(N_Z * GROUP, E)
        return jnp.dot(own_counts[:, columns], rows, preferred_element_type=F32)

    own_side = product(core)

    def wait_core(where, _):
        grads_over(where, 1 - core).wait_recv()
        return 0

    lax.fori_loop(0, N_Z, wait_core, 0)
    table_grad_ref[...] = own_side + product(1 - core)

    def drain_z(s, _):
        z_copy(ids_all.at[core, z], ids_all.at[core, z], ids_send, ids_recv, s).wait_send()
        z_copy(pooled_out, pooled_in.at[core, z], pooled_send, pooled_recv, s).wait_send()
        z_copy(grad_pair.at[0], grad_in.at[z], grad_send, grad_recv, s).wait_send()
        z_copy(quarter(z, x), quarter(z, x), z_send, z_recv, s).wait_send()
        return 0

    def drain_x(where, _):
        for step in range(1, N_X):
            x_copy(where, x, step).wait_send()
        grads_over(where, core).wait_send()
        return 0

    for s in range(1, N_Y):
        y_copy(s).wait_send()
    for step in ROW_STEPS:
        row_copy(partial_out.at[0], partial_in.at[k], partial_send, partial_recv, step).wait_send()
    lax.fori_loop(1, N_Z, drain_z, 0)
    lax.fori_loop(0, N_Z, drain_x, 0)
    ids_over.wait_send()
    pooled_over.wait_send()
    grad_over.wait_send()


def hand_over(table_grad_hbm, item_grad_hbm, table_grad_out, item_grad_out, table_grad, item_grad, sem):
    parts = []
    for n, (source, held, target) in enumerate(
        [(table_grad_hbm, table_grad, table_grad_out), (item_grad_hbm, item_grad, item_grad_out)]
    ):
        for part in range(2):
            rows = pl.ds(part * 128, 128)
            parts.append(
                (
                    pltpu.make_async_copy(source.at[rows], held.at[rows], sem.at[0, n, part]),
                    pltpu.make_async_copy(held.at[rows], target.at[rows], sem.at[1, n, part]),
                )
            )
    for load, _ in parts:
        load.start()
    for load, store in parts:
        load.wait()
        store.start()
    for _, store in parts:
        store.wait()


def per_device(user_table, user_ids, item_features, counts, placement, labels, w_hidden, bias, w_out):
    vmem = pl.BlockSpec(memory_space=pltpu.VMEM)
    hbm = pl.BlockSpec(memory_space=pl.ANY)
    dma = pltpu.SemaphoreType.DMA
    outs = (jax.ShapeDtypeStruct((SHARE, E), F32), jax.ShapeDtypeStruct((CAND, E), BF16))
    grads = pl.pallas_call(
        kernel,
        out_shape=outs,
        in_specs=[hbm] * 8 + [vmem],
        out_specs=(vmem, vmem),
        scratch_shapes=[
            pltpu.VMEM((ROWS, E), BF16),
            pltpu.VMEM((3 * E, H), BF16),
            pltpu.VMEM((BAG, GROUP), jnp.int32),
            pltpu.VMEM((CAND, E), BF16),
            pltpu.VMEM((1, COLUMN), jnp.int32),
            pltpu.VMEM((1, COLUMN), jnp.int32),
            pltpu.VMEM((1, CAND), jnp.int32),
            pltpu.VMEM((1, H), F32),
            pltpu.VMEM((GROUP, ROWS), BF16),
            pltpu.VMEM((N_ROW, 8, 128), F32),
            pltpu.VMEM((N_ROW, 8, 128), F32),
            pltpu.VMEM((8, 128), F32),
            pltpu.VMEM((2, N_Z, 8, 128), F32),
            pltpu.VMEM((128, E), BF16),
            pltpu.VMEM((2, N_Z, 8, 128), F32),
            pltpu.VMEM((N_Z, 8, 128), F32),
            pltpu.VMEM((N_Z, 8, 128), F32),
            pltpu.VMEM((N_Z, 8, 128), F32),
            pltpu.VMEM((8, 128), F32),
            pltpu.VMEM((N_Y, 8, 128), F32),
            pltpu.VMEM((2, N_Z, BAG, GROUP), jnp.int16),
            pltpu.VMEM((SHARE, N_DP * GROUP), BF16),
            pltpu.VMEM((2, N_Z, GROUP, E), BF16),
            dma((8,)),
            dma((N_Z,)),
            dma((N_Z,)),
            dma((N_ROW,)),
            dma((N_ROW,)),
            dma((N_Z,)),
            dma((N_Z,)),
            dma((N_Z,)),
            dma((N_Z,)),
            dma((N_Y,)),
            dma((N_Y,)),
            dma((N_Z,)),
            dma((N_Z,)),
            dma((N_Z, N_X)),
            dma((N_Z, N_X)),
            dma((3 + N_Z,)),
            dma((3 + N_Z,)),
        ],
        compiler_params=pltpu.CompilerParams(
            collective_id=0, has_side_effects=True, vmem_limit_bytes=60 * 1024 * 1024
        ),
    )(
        user_table,
        user_ids.T,
        item_features,
        counts,
        placement,
        labels.reshape(1, CAND),
        w_hidden,
        bias.reshape(1, H),
        w_out,
    )
    return pl.pallas_call(
        hand_over,
        out_shape=outs,
        in_specs=[hbm] * 2,
        out_specs=(hbm, hbm),
        scratch_shapes=[pltpu.VMEM((SHARE, E), F32), pltpu.VMEM((CAND, E), BF16), dma((2, 2, 2))],
        compiler_params=pltpu.CompilerParams(vmem_limit_bytes=60 * 1024 * 1024),
    )(*grads)


def solution(mesh):
    return jax.shard_map(
        per_device,
        mesh=mesh,
        in_specs=(
            P("row", None),
            P("dp", None),
            P(("dp", "row"), None),
            P("row", None),
            P("row", None),
            P(("dp", "row")),
            P(),
            P(),
            P(),
        ),
        out_specs=(P(("row", "dp"), None), P(("dp", "row"), None)),
        check_vma=False,
    )
```

```python
import functools

import jax
import jax.numpy as jnp
from jax import lax
from jax.experimental import pallas as pl
from jax.experimental.pallas import tpu as pltpu
from jax.sharding import PartitionSpec as P

MESH = pl.DeviceIdType.MESH
loss_scale = 64.0

N_DP = 24
N_ROW = 32
N_X = 4
N_Z = 12
REQ = 4
GROUP = N_ROW * REQ
COLUMN = N_DP * REQ
BAG = 32
E = 256
H = 1024
ROWS = 6144
SHARE = ROWS // N_DP
CAND = 256
QUARTER = GROUP // N_X
N_Y = N_ROW // N_X
BLOCK = 16
N_BLOCK = GROUP // BLOCK
BF16 = jnp.bfloat16
F32 = jnp.float32


def iota(shape, dim, dtype=jnp.int32):
    return lax.broadcasted_iota(jnp.int32, shape, dim).astype(dtype)


ROW_STEPS = [(v, u) for v in (4, 3, 5, 2, 6, 1, 7, 0) for u in (2, 1, 3, 0) if (v, u) != (0, 0)]


def to_messages(rows):
    n = rows.shape[0] // 8
    left = rows[:, :128].reshape(n, 8, 128)
    right = rows[:, 128:].reshape(n, 8, 128)
    upper = iota((n, 8, 128), 1) < 4
    even = jnp.where(upper, left, pltpu.roll(right, 4, axis=1))
    odd = jnp.where(upper, pltpu.roll(left, 4, axis=1), right)
    return jnp.stack([even, odd], axis=1).reshape(2 * n, 8, 128)


def from_messages(messages):
    n = messages.shape[0] // 2
    pairs = messages.reshape(n, 2, 8, 128)
    even, odd = pairs[:, 0], pairs[:, 1]
    upper = iota((n, 8, 128), 1) < 4
    left = jnp.where(upper, even, pltpu.roll(odd, 4, axis=1))
    right = jnp.where(upper, pltpu.roll(even, 4, axis=1), odd)
    return left.reshape(8 * n, 128), right.reshape(8 * n, 128)


def wrap(value, size):
    return jnp.where(value >= size, value - size, value)


def alternate(s, size):
    half = (s + 1) // 2
    return jnp.where(s % 2 == 1, half, wrap(size - half, size))


def flatten(turned):
    lag = (iota((8, 128), 0) + 8 - iota((8, 128), 1) // BLOCK) % 8
    parts = []
    for first in range(0, BAG, 8):
        tile = turned[first : first + 8]
        part = tile
        for d in range(1, 8):
            moved = pltpu.roll(pltpu.roll(tile, d, axis=0), 128 - BLOCK * d, axis=1)
            part = jnp.where(lag == d, moved, part)
        parts.append(part)
    return jnp.concatenate(parts, axis=1)


def kernel(
    table_hbm,
    ids_hbm,
    item_hbm,
    counts_hbm,
    placement_hbm,
    labels_hbm,
    w_hidden_hbm,
    bias_hbm,
    w_out_ref,
    table_grad_ref,
    item_grad_ref,
    table,
    w_hidden,
    ids_ref,
    item_ref,
    counts_ref,
    placement_ref,
    labels_ref,
    bias_ref,
    group_counts,
    partial_out,
    partial_in,
    pooled_out,
    pooled_in,
    pooled_column,
    grad_out,
    grad_core,
    grad_pair,
    grad_in,
    request_out,
    request_in,
    ids_all,
    chip_counts,
    all_grads,
    parts,
    part_out,
    part_in,
    load_sem,
    ids_send,
    ids_recv,
    partial_send,
    partial_recv,
    pooled_send,
    pooled_recv,
    grad_send,
    grad_recv,
    request_send,
    request_recv,
    z_send,
    z_recv,
    x_send,
    x_recv,
    core_send,
    core_recv,
):
    i = lax.axis_index("dp")
    k = lax.axis_index("row")
    z = i // 2
    core = i % 2
    y = k // N_X
    x = k % N_X

    ids_load = pltpu.make_async_copy(ids_hbm, ids_ref, load_sem.at[0])
    table_load = pltpu.make_async_copy(table_hbm, table, load_sem.at[1])
    later_loads = [
        pltpu.make_async_copy(source, target, load_sem.at[n])
        for n, (source, target) in enumerate(
            [
                (placement_hbm, placement_ref),
                (counts_hbm, counts_ref),
                (labels_hbm, labels_ref),
                (item_hbm, item_ref),
                (bias_hbm, bias_ref),
                (w_hidden_hbm, w_hidden),
            ],
            2,
        )
    ]
    ids_load.start()
    table_load.start()
    for load in later_loads:
        load.start()

    barrier = pltpu.get_barrier_semaphore()

    def in_row(step):
        return (y + step[0]) % N_Y * N_X + (x + step[1]) % N_X

    def greet_z(s, _):
        there = wrap(z + alternate(N_Z - s, N_Z), N_Z) * 2 + core
        pl.semaphore_signal(barrier, inc=1, device_id=(there, k), device_id_type=MESH)
        return 0

    def greet_row(steps):
        for step in steps:
            pl.semaphore_signal(barrier, inc=1, device_id=(i, in_row(step)), device_id_type=MESH)

    greet_row(ROW_STEPS[:12])
    lax.fori_loop(1, N_Z, greet_z, 0)
    greet_row(ROW_STEPS[12:])
    pl.semaphore_signal(barrier, inc=1, device_id=(z * 2 + 1 - core, k), device_id_type=MESH)

    ids_load.wait()
    relative = ids_ref[...] - k * ROWS
    relative = jnp.where((relative >= 0) & (relative < ROWS), relative, -1)
    flat = flatten(relative)
    in_block = iota((N_BLOCK, BLOCK * BAG), 1) % BLOCK
    high_key = jnp.where(flat >= 0, (flat >> 8) * BLOCK + in_block, -1)
    low_key = flat & (SHARE - 1)
    high_row = iota((N_DP * BLOCK, 1), 0)
    low_row = iota((SHARE, 1), 0)
    for b in range(N_BLOCK):
        high = jnp.where(high_key[b : b + 1] == high_row, 1.0, 0.0).astype(BF16)
        low = jnp.where(low_key[b : b + 1] == low_row, 1.0, 0.0).astype(BF16)
        found = lax.dot_general(high, low, (((1,), (1,)), ((), ())), preferred_element_type=F32).astype(BF16)
        for h in range(N_DP):
            group_counts[b * BLOCK : (b + 1) * BLOCK, h * SHARE : (h + 1) * SHARE] = found[
                h * BLOCK : (h + 1) * BLOCK
            ]
    table_load.wait()
    partial = jnp.dot(group_counts[...], table[...], preferred_element_type=F32)
    partial_out[...] = to_messages(partial)

    pl.semaphore_wait(barrier, N_ROW - 1 + N_Z)

    def row_copy(src, dst, send, recv, step):
        return pltpu.make_async_remote_copy(
            src_ref=src,
            dst_ref=dst,
            send_sem=send.at[step[0] * N_X + step[1]],
            recv_sem=recv.at[k],
            device_id=(i, in_row(step)),
            device_id_type=MESH,
        )

    def z_copy(src, dst, send, recv, s):
        return pltpu.make_async_remote_copy(
            src_ref=src,
            dst_ref=dst,
            send_sem=send.at[s],
            recv_sem=recv.at[z],
            device_id=(wrap(z + s, N_Z) * 2 + core, k),
            device_id_type=MESH,
        )

    def core_copy(src, dst, n):
        return pltpu.make_async_remote_copy(
            src_ref=src,
            dst_ref=dst,
            send_sem=core_send.at[n],
            recv_sem=core_recv.at[n],
            device_id=(z * 2 + 1 - core, k),
            device_id_type=MESH,
        )

    def arrived(buffer, recv, source):
        pltpu.make_async_copy(buffer.at[source], buffer.at[source], recv.at[source]).wait()

    for step in ROW_STEPS:
        row_copy(partial_out.at[in_row(step)], partial_in.at[k], partial_send, partial_recv, step).start()
    partial_in[k] = partial_out[k]

    to = iota((GROUP, GROUP), 1)
    moved_from = (to % QUARTER // REQ) * (N_X * REQ) + to // QUARTER * REQ + to % REQ
    reorder = jnp.where(iota((GROUP, GROUP), 0) == moved_from, 1.0, 0.0).astype(BF16)
    high_digit = (relative >> 8).astype(F32).astype(BF16)
    low_digit = (relative & (SHARE - 1)).astype(F32).astype(BF16)
    ids_moved = jnp.dot(high_digit, reorder, preferred_element_type=F32) * SHARE + jnp.dot(
        low_digit, reorder, preferred_element_type=F32
    )
    ids_all[z] = ids_moved.astype(jnp.int32).astype(jnp.int16)

    def send_ids(s, _):
        z_copy(ids_all.at[z], ids_all.at[z], ids_send, ids_recv, alternate(s, N_Z)).start()
        return 0

    lax.fori_loop(1, N_Z, send_ids, 0)

    def count_group(n):
        where, side = wrap(z + alternate(n // 2, N_Z), N_Z), n % 2
        first = (z * 2 + side) * SHARE
        ids = jnp.clip(ids_all[where].astype(jnp.int32) - first, -1, SHARE).astype(F32)
        row = iota((SHARE, GROUP), 0, F32).astype(BF16)
        total = jnp.zeros((SHARE, GROUP), BF16)
        one, zero = jnp.ones((), BF16), jnp.zeros((), BF16)
        for b in range(BAG):
            wanted = jnp.broadcast_to(ids[b : b + 1], (16, GROUP)).astype(BF16)
            total = total + jnp.where(jnp.tile(wanted, (SHARE // 16, 1)) == row, one, zero)
        columns = pl.ds(pl.multiple_of(where * GROUP, GROUP), GROUP)
        chip_counts[side, :, columns] = total

    def count_step(n, _):
        count_group(n)
        return 0

    for load in later_loads:
        load.wait()
    padding = jnp.zeros((1, 128 - COLUMN), jnp.int32)
    order = jnp.concatenate([placement_ref[...], padding - 1], axis=1)
    column_counts = jnp.concatenate([counts_ref[...], padding], axis=1).astype(F32)
    eye = iota((128, 128), 0) == iota((128, 128), 1)
    place_at = jnp.where(order == iota((128, 128), 0), iota((128, 128), 1).astype(F32), 0.0)
    position = jnp.sum(place_at, axis=1, keepdims=True)
    position_row = jnp.sum(jnp.where(eye, position, 0.0), axis=0, keepdims=True)
    start = jnp.sum(jnp.where(position_row < position, column_counts, 0.0), axis=1, keepdims=True)
    count = jnp.sum(jnp.where(eye, column_counts, 0.0), axis=1, keepdims=True)
    start_row = jnp.sum(jnp.where(eye, start, 0.0), axis=0, keepdims=True)
    end, end_row = start + count, start_row + column_counts
    first = (i * CAND).astype(F32)
    slot = first + iota((CAND, 1), 0, F32)
    slot_row = first + iota((1, CAND), 1, F32)
    member = jnp.where((slot >= start_row) & (slot < end_row), 1.0, 0.0).astype(BF16)
    member_turned = jnp.where((slot_row >= start) & (slot_row < end), 1.0, 0.0).astype(BF16)
    diagonal = iota((CAND, CAND), 0) == iota((CAND, CAND), 1)
    label = jnp.sum(jnp.where(diagonal, labels_ref[...].astype(F32), 0.0), axis=1, keepdims=True)

    item = item_ref[...]
    item_wide = item.astype(F32)
    item_pre = jnp.dot(item, w_hidden[E : 2 * E], preferred_element_type=F32) + bias_ref[...]

    lax.fori_loop(0, 2, count_step, 0)

    def wait_partial(s, _):
        arrived(partial_in, partial_recv, (k + s) % N_ROW)
        return 0

    lax.fori_loop(1, N_ROW, wait_partial, 0)
    pooled = jnp.sum(partial_in[...], axis=0)
    pooled_out[...] = pooled
    pooled_in[core, z] = pooled

    def send_pooled(s, _):
        z_copy(pooled_out, pooled_in.at[core, z], pooled_send, pooled_recv, alternate(N_Z - s, N_Z)).start()
        return 0

    def wait_ids(s, _):
        where = wrap(z + s, N_Z)
        arrived(ids_all, ids_recv, where)
        return 0

    def wait_pooled(s, _):
        where = wrap(z + s, N_Z)
        block = pooled_in.at[core, where]
        pltpu.make_async_copy(block, block, pooled_recv.at[where]).wait()
        return 0

    lax.fori_loop(1, N_Z, send_pooled, 0)
    pooled_column[...] = jnp.zeros_like(pooled_column)
    lax.fori_loop(1, N_Z, wait_ids, 0)
    lax.fori_loop(2, 11, count_step, 0)
    lax.fori_loop(1, N_Z, wait_pooled, 0)
    pooled_over = core_copy(pooled_in.at[core], pooled_in.at[core], 1)
    pooled_over.start()
    pooled_over.wait_recv()
    pooled_all = jnp.stack([pooled_in[0], pooled_in[1]], axis=1).reshape(N_DP, 8, 128)
    left, right = from_messages(pooled_all)
    pooled_column[:COLUMN, :128] = left.astype(BF16)
    pooled_column[:COLUMN, 128:] = right.astype(BF16)

    user_rows = jnp.dot(member, pooled_column[...], preferred_element_type=F32)
    user = user_rows.astype(BF16)
    both = (user_rows * item_wide).astype(BF16)
    pre = (
        item_pre
        + jnp.dot(user, w_hidden[:E], preferred_element_type=F32)
        + jnp.dot(both, w_hidden[2 * E :], preferred_element_type=F32)
    )
    sigma = jax.nn.sigmoid(pre)
    hidden = (pre * sigma).astype(BF16).astype(F32)
    w_out = w_out_ref[...].astype(F32).reshape(1, H)
    score = jnp.sum(hidden * w_out, axis=1, keepdims=True)
    dscore = loss_scale * (jax.nn.sigmoid(score) - label)
    slope = sigma * (1.0 + pre * (1.0 - sigma))
    dhidden = (dscore * w_out * slope).astype(BF16)
    dfeatures = lax.dot_general(dhidden, w_hidden[...], (((1,), (1,)), ((), ())), preferred_element_type=F32)
    user_grad = dfeatures[:, :E] + dfeatures[:, 2 * E :] * item_wide
    coarse = user_grad.astype(BF16)
    fine = (user_grad - coarse.astype(F32)).astype(BF16)
    column_grad = jnp.dot(member_turned, coarse, preferred_element_type=F32) + jnp.dot(
        member_turned, fine, preferred_element_type=F32
    )
    by_core = to_messages(column_grad[:COLUMN]).reshape(N_Z, 2, 8, 128)
    grad_out[0] = by_core[:, 0]
    grad_out[1] = by_core[:, 1]

    grad_over = core_copy(grad_out.at[1 - core], grad_core, 2)
    grad_over.start()
    item_grad_ref[...] = (dfeatures[:, E : 2 * E] + dfeatures[:, 2 * E :] * user_rows).astype(BF16)
    grad_over.wait_recv()
    grad_pair[...] = grad_out[core] + grad_core[...]

    def send_grad(s, _):
        step = alternate(N_Z - s, N_Z)
        z_copy(grad_pair.at[wrap(z + step, N_Z)], grad_in.at[z], grad_send, grad_recv, step).start()
        return 0

    def wait_grad(s, _):
        arrived(grad_in, grad_recv, wrap(z + s, N_Z))
        return 0

    lax.fori_loop(1, N_Z, send_grad, 0)
    grad_in[z] = grad_pair[z]
    lax.fori_loop(11, 19, count_step, 0)
    lax.fori_loop(1, N_Z, wait_grad, 0)
    request_grad = jnp.sum(grad_in[...], axis=0)
    request_out[...] = request_grad
    request_in[y] = request_grad

    def y_copy(s):
        return pltpu.make_async_remote_copy(
            src_ref=request_out,
            dst_ref=request_in.at[y],
            send_sem=request_send.at[s],
            recv_sem=request_recv.at[y],
            device_id=(i, (k + s * N_X) % N_ROW),
            device_id_type=MESH,
        )

    for s in (4, 3, 5, 2, 6, 1, 7):
        y_copy(s).start()
    lax.fori_loop(19, 22, count_step, 0)
    for s in range(1, N_Y):
        arrived(request_in, request_recv, (y + s) % N_Y)
    left, right = from_messages(request_in[...])
    own_rows = pl.ds(pl.multiple_of(x * QUARTER, QUARTER), QUARTER)
    all_grads[z, own_rows, :128] = left.astype(BF16)
    all_grads[z, own_rows, 128:] = right.astype(BF16)

    def quarter(where, which):
        return all_grads.at[where, pl.ds(pl.multiple_of(which * QUARTER, QUARTER), QUARTER)]

    def send_z(s, _):
        z_copy(quarter(z, x), quarter(z, x), z_send, z_recv, alternate(s, N_Z)).start()
        return 0

    def x_copy(where, which, s):
        return pltpu.make_async_remote_copy(
            src_ref=quarter(where, which),
            dst_ref=quarter(where, which),
            send_sem=x_send.at[where, s],
            recv_sem=x_recv.at[where, which],
            device_id=(i, y * N_X + (x + s) % N_X),
            device_id_type=MESH,
        )

    lax.fori_loop(1, N_Z, send_z, 0)
    for step in range(1, N_X):
        x_copy(z, x, step).start()
    lax.fori_loop(22, 24, count_step, 0)

    def pass_on(s, _):
        where = wrap(z + alternate(s, N_Z), N_Z)
        block = quarter(where, x)
        pltpu.make_async_copy(block, block, z_recv.at[where]).wait()
        for step in range(1, N_X):
            x_copy(where, x, step).start()
        return 0

    lax.fori_loop(1, N_Z, pass_on, 0)

    def product(where, side):
        columns = pl.ds(pl.multiple_of(where * GROUP, GROUP), GROUP)
        return jnp.dot(chip_counts[side, :, columns], all_grads[where], preferred_element_type=F32)

    def wait_x(s):
        where = wrap(z + alternate(s, N_Z), N_Z)
        for step in range(1, N_X):
            which = (x + step) % N_X
            block = quarter(where, which)
            pltpu.make_async_copy(block, block, x_recv.at[where, which]).wait()
        return where

    def add_group(s, _):
        where = wait_x(s)
        for side in range(2):
            parts[side] = parts[side] + product(where, side)
        return 0

    parts[...] = jnp.zeros_like(parts)
    lax.fori_loop(0, N_Z - 1, add_group, 0)
    last = wait_x(N_Z - 1)
    part_out[...] = (parts[1 - core] + product(last, 1 - core)).astype(BF16)
    part_over = core_copy(part_out, part_in, 3)
    part_over.start()
    own_part = parts[core] + product(last, core)
    part_over.wait_recv()
    table_grad_ref[...] = own_part + part_in[...].astype(F32)

    def drain_z(s, _):
        z_copy(ids_all.at[z], ids_all.at[z], ids_send, ids_recv, s).wait_send()
        z_copy(pooled_out, pooled_in.at[core, z], pooled_send, pooled_recv, s).wait_send()
        z_copy(grad_pair.at[0], grad_in.at[z], grad_send, grad_recv, s).wait_send()
        z_copy(quarter(z, x), quarter(z, x), z_send, z_recv, s).wait_send()
        return 0

    def drain_x(where, _):
        for step in range(1, N_X):
            x_copy(where, x, step).wait_send()
        return 0

    for s in range(1, N_Y):
        y_copy(s).wait_send()
    for step in ROW_STEPS:
        row_copy(partial_out.at[0], partial_in.at[k], partial_send, partial_recv, step).wait_send()
    lax.fori_loop(1, N_Z, drain_z, 0)
    lax.fori_loop(0, N_Z, drain_x, 0)
    part_over.wait_send()
    pooled_over.wait_send()
    grad_over.wait_send()


def hand_over(table_grad_hbm, item_grad_hbm, table_grad_out, item_grad_out, table_grad, item_grad, sem):
    parts = []
    for n, (source, held, target) in enumerate(
        [(table_grad_hbm, table_grad, table_grad_out), (item_grad_hbm, item_grad, item_grad_out)]
    ):
        for part in range(2):
            rows = pl.ds(part * 128, 128)
            parts.append(
                (
                    pltpu.make_async_copy(source.at[rows], held.at[rows], sem.at[0, n, part]),
                    pltpu.make_async_copy(held.at[rows], target.at[rows], sem.at[1, n, part]),
                )
            )
    for load, _ in parts:
        load.start()
    for load, store in parts:
        load.wait()
        store.start()
    for _, store in parts:
        store.wait()


def per_device(user_table, user_ids, item_features, counts, placement, labels, w_hidden, bias, w_out):
    vmem = pl.BlockSpec(memory_space=pltpu.VMEM)
    hbm = pl.BlockSpec(memory_space=pl.ANY)
    dma = pltpu.SemaphoreType.DMA
    outs = (jax.ShapeDtypeStruct((SHARE, E), F32), jax.ShapeDtypeStruct((CAND, E), BF16))
    grads = pl.pallas_call(
        kernel,
        out_shape=outs,
        in_specs=[hbm] * 8 + [vmem],
        out_specs=(vmem, vmem),
        scratch_shapes=[
            pltpu.VMEM((ROWS, E), BF16),
            pltpu.VMEM((3 * E, H), BF16),
            pltpu.VMEM((BAG, GROUP), jnp.int32),
            pltpu.VMEM((CAND, E), BF16),
            pltpu.VMEM((1, COLUMN), jnp.int32),
            pltpu.VMEM((1, COLUMN), jnp.int32),
            pltpu.VMEM((1, CAND), jnp.int32),
            pltpu.VMEM((1, H), F32),
            pltpu.VMEM((GROUP, ROWS), BF16),
            pltpu.VMEM((N_ROW, 8, 128), F32),
            pltpu.VMEM((N_ROW, 8, 128), F32),
            pltpu.VMEM((8, 128), F32),
            pltpu.VMEM((2, N_Z, 8, 128), F32),
            pltpu.VMEM((128, E), BF16),
            pltpu.VMEM((2, N_Z, 8, 128), F32),
            pltpu.VMEM((N_Z, 8, 128), F32),
            pltpu.VMEM((N_Z, 8, 128), F32),
            pltpu.VMEM((N_Z, 8, 128), F32),
            pltpu.VMEM((8, 128), F32),
            pltpu.VMEM((N_Y, 8, 128), F32),
            pltpu.VMEM((N_Z, BAG, GROUP), jnp.int16),
            pltpu.VMEM((2, SHARE, N_Z * GROUP), BF16),
            pltpu.VMEM((N_Z, GROUP, E), BF16),
            pltpu.VMEM((2, SHARE, E), F32),
            pltpu.VMEM((SHARE, E), BF16),
            pltpu.VMEM((SHARE, E), BF16),
            dma((8,)),
            dma((N_Z,)),
            dma((N_Z,)),
            dma((N_ROW,)),
            dma((N_ROW,)),
            dma((N_Z,)),
            dma((N_Z,)),
            dma((N_Z,)),
            dma((N_Z,)),
            dma((N_Y,)),
            dma((N_Y,)),
            dma((N_Z,)),
            dma((N_Z,)),
            dma((N_Z, N_X)),
            dma((N_Z, N_X)),
            dma((4,)),
            dma((4,)),
        ],
        compiler_params=pltpu.CompilerParams(
            collective_id=0, has_side_effects=True, vmem_limit_bytes=60 * 1024 * 1024
        ),
    )(
        user_table,
        user_ids.T,
        item_features,
        counts,
        placement,
        labels.reshape(1, CAND),
        w_hidden,
        bias.reshape(1, H),
        w_out,
    )
    return pl.pallas_call(
        hand_over,
        out_shape=outs,
        in_specs=[hbm] * 2,
        out_specs=(hbm, hbm),
        scratch_shapes=[pltpu.VMEM((SHARE, E), F32), pltpu.VMEM((CAND, E), BF16), dma((2, 2, 2))],
        compiler_params=pltpu.CompilerParams(vmem_limit_bytes=60 * 1024 * 1024),
    )(*grads)


def solution(mesh):
    return jax.shard_map(
        per_device,
        mesh=mesh,
        in_specs=(
            P("row", None),
            P("dp", None),
            P(("dp", "row"), None),
            P("row", None),
            P("row", None),
            P(("dp", "row")),
            P(),
            P(),
            P(),
        ),
        out_specs=(P(("row", "dp"), None), P(("dp", "row"), None)),
        check_vma=False,
    )
```

```python
import functools

import jax
import jax.numpy as jnp
from jax import lax
from jax.experimental import pallas as pl
from jax.experimental.pallas import tpu as pltpu
from jax.sharding import PartitionSpec as P

MESH = pl.DeviceIdType.MESH
loss_scale = 64.0

N_DP = 24
N_ROW = 32
N_X = 4
N_Z = 12
REQ = 4
GROUP = N_ROW * REQ
COLUMN = N_DP * REQ
BAG = 32
E = 256
H = 1024
ROWS = 6144
SHARE = ROWS // N_DP
CAND = 256
QUARTER = GROUP // N_X
N_Y = N_ROW // N_X
BLOCK = 16
N_BLOCK = GROUP // BLOCK
BF16 = jnp.bfloat16
F32 = jnp.float32


def iota(shape, dim, dtype=jnp.int32):
    return lax.broadcasted_iota(jnp.int32, shape, dim).astype(dtype)


ROW_STEPS = [(v, u) for v in (4, 3, 5, 2, 6, 1, 7, 0) for u in (2, 1, 3, 0) if (v, u) != (0, 0)]


def to_messages(rows):
    n = rows.shape[0] // 8
    left = rows[:, :128].reshape(n, 8, 128)
    right = rows[:, 128:].reshape(n, 8, 128)
    upper = iota((n, 8, 128), 1) < 4
    even = jnp.where(upper, left, pltpu.roll(right, 4, axis=1))
    odd = jnp.where(upper, pltpu.roll(left, 4, axis=1), right)
    return jnp.stack([even, odd], axis=1).reshape(2 * n, 8, 128)


def from_messages(messages):
    n = messages.shape[0] // 2
    pairs = messages.reshape(n, 2, 8, 128)
    even, odd = pairs[:, 0], pairs[:, 1]
    upper = iota((n, 8, 128), 1) < 4
    left = jnp.where(upper, even, pltpu.roll(odd, 4, axis=1))
    right = jnp.where(upper, pltpu.roll(even, 4, axis=1), odd)
    return left.reshape(8 * n, 128), right.reshape(8 * n, 128)


def wrap(value, size):
    return jnp.where(value >= size, value - size, value)


def alternate(s, size):
    half = (s + 1) // 2
    return jnp.where(s % 2 == 1, half, wrap(size - half, size))


def flatten(turned):
    lag = (iota((8, 128), 0) + 8 - iota((8, 128), 1) // BLOCK) % 8
    parts = []
    for first in range(0, BAG, 8):
        tile = turned[first : first + 8]
        part = tile
        for d in range(1, 8):
            moved = pltpu.roll(pltpu.roll(tile, d, axis=0), 128 - BLOCK * d, axis=1)
            part = jnp.where(lag == d, moved, part)
        parts.append(part)
    return jnp.concatenate(parts, axis=1)


def kernel(
    table_hbm,
    ids_hbm,
    item_hbm,
    counts_hbm,
    placement_hbm,
    labels_hbm,
    w_hidden_hbm,
    bias_hbm,
    w_out_ref,
    table_grad_hbm,
    item_grad_hbm,
    table_grad_ref,
    item_grad_ref,
    table,
    w_hidden,
    ids_ref,
    item_ref,
    counts_ref,
    placement_ref,
    labels_ref,
    bias_ref,
    group_counts,
    partial_out,
    partial_in,
    pooled_out,
    pooled_in,
    pooled_column,
    grad_out,
    grad_core,
    grad_pair,
    grad_in,
    request_out,
    request_in,
    ids_all,
    chip_counts,
    all_grads,
    parts,
    part_out,
    part_in,
    load_sem,
    store_sem,
    ids_send,
    ids_recv,
    partial_send,
    partial_recv,
    pooled_send,
    pooled_recv,
    grad_send,
    grad_recv,
    request_send,
    request_recv,
    z_send,
    z_recv,
    x_send,
    x_recv,
    core_send,
    core_recv,
):
    i = lax.axis_index("dp")
    k = lax.axis_index("row")
    z = i // 2
    core = i % 2
    y = k // N_X
    x = k % N_X

    ids_load = pltpu.make_async_copy(ids_hbm, ids_ref, load_sem.at[0])
    table_load = pltpu.make_async_copy(table_hbm, table, load_sem.at[1])
    later_loads = [
        pltpu.make_async_copy(source, target, load_sem.at[n])
        for n, (source, target) in enumerate(
            [
                (placement_hbm, placement_ref),
                (counts_hbm, counts_ref),
                (labels_hbm, labels_ref),
                (item_hbm, item_ref),
                (bias_hbm, bias_ref),
                (w_hidden_hbm, w_hidden),
            ],
            2,
        )
    ]
    ids_load.start()
    table_load.start()
    for load in later_loads:
        load.start()

    barrier = pltpu.get_barrier_semaphore()

    def in_row(step):
        return (y + step[0]) % N_Y * N_X + (x + step[1]) % N_X

    def greet_z(s, _):
        there = wrap(z + alternate(N_Z - s, N_Z), N_Z) * 2 + core
        pl.semaphore_signal(barrier, inc=1, device_id=(there, k), device_id_type=MESH)
        return 0

    def greet_row(steps):
        for step in steps:
            pl.semaphore_signal(barrier, inc=1, device_id=(i, in_row(step)), device_id_type=MESH)

    greet_row(ROW_STEPS[:12])
    lax.fori_loop(1, N_Z, greet_z, 0)
    greet_row(ROW_STEPS[12:])
    pl.semaphore_signal(barrier, inc=1, device_id=(z * 2 + 1 - core, k), device_id_type=MESH)

    ids_load.wait()
    relative = ids_ref[...] - k * ROWS
    relative = jnp.where((relative >= 0) & (relative < ROWS), relative, -1)
    flat = flatten(relative)
    in_block = iota((N_BLOCK, BLOCK * BAG), 1) % BLOCK
    high_key = jnp.where(flat >= 0, (flat >> 8) * BLOCK + in_block, -1)
    low_key = flat & (SHARE - 1)
    high_row = iota((N_DP * BLOCK, 1), 0)
    low_row = iota((SHARE, 1), 0)
    for b in range(N_BLOCK):
        high = jnp.where(high_key[b : b + 1] == high_row, 1.0, 0.0).astype(BF16)
        low = jnp.where(low_key[b : b + 1] == low_row, 1.0, 0.0).astype(BF16)
        found = lax.dot_general(high, low, (((1,), (1,)), ((), ())), preferred_element_type=F32).astype(BF16)
        for h in range(N_DP):
            group_counts[b * BLOCK : (b + 1) * BLOCK, h * SHARE : (h + 1) * SHARE] = found[
                h * BLOCK : (h + 1) * BLOCK
            ]
    table_load.wait()
    partial = jnp.dot(group_counts[...], table[...], preferred_element_type=F32)
    partial_out[...] = to_messages(partial)

    pl.semaphore_wait(barrier, N_ROW - 1 + N_Z)

    def row_copy(src, dst, send, recv, step):
        return pltpu.make_async_remote_copy(
            src_ref=src,
            dst_ref=dst,
            send_sem=send.at[step[0] * N_X + step[1]],
            recv_sem=recv.at[k],
            device_id=(i, in_row(step)),
            device_id_type=MESH,
        )

    def z_copy(src, dst, send, recv, s):
        return pltpu.make_async_remote_copy(
            src_ref=src,
            dst_ref=dst,
            send_sem=send.at[s],
            recv_sem=recv.at[z],
            device_id=(wrap(z + s, N_Z) * 2 + core, k),
            device_id_type=MESH,
        )

    def core_copy(src, dst, n):
        return pltpu.make_async_remote_copy(
            src_ref=src,
            dst_ref=dst,
            send_sem=core_send.at[n],
            recv_sem=core_recv.at[n],
            device_id=(z * 2 + 1 - core, k),
            device_id_type=MESH,
        )

    def arrived(buffer, recv, source):
        pltpu.make_async_copy(buffer.at[source], buffer.at[source], recv.at[source]).wait()

    for step in ROW_STEPS:
        row_copy(partial_out.at[in_row(step)], partial_in.at[k], partial_send, partial_recv, step).start()
    partial_in[k] = partial_out[k]

    to = iota((GROUP, GROUP), 1)
    moved_from = (to % QUARTER // REQ) * (N_X * REQ) + to // QUARTER * REQ + to % REQ
    reorder = jnp.where(iota((GROUP, GROUP), 0) == moved_from, 1.0, 0.0).astype(BF16)
    high_digit = (relative >> 8).astype(F32).astype(BF16)
    low_digit = (relative & (SHARE - 1)).astype(F32).astype(BF16)
    ids_moved = jnp.dot(high_digit, reorder, preferred_element_type=F32) * SHARE + jnp.dot(
        low_digit, reorder, preferred_element_type=F32
    )
    ids_all[z] = ids_moved.astype(jnp.int32).astype(jnp.int16)

    def send_ids(s, _):
        z_copy(ids_all.at[z], ids_all.at[z], ids_send, ids_recv, alternate(s, N_Z)).start()
        return 0

    lax.fori_loop(1, N_Z, send_ids, 0)

    def count_group(n):
        where, side = wrap(z + alternate(n // 2, N_Z), N_Z), n % 2
        first = (z * 2 + side) * SHARE
        ids = jnp.clip(ids_all[where].astype(jnp.int32) - first, -1, SHARE).astype(F32)
        row = iota((SHARE, GROUP), 0, F32).astype(BF16)
        total = jnp.zeros((SHARE, GROUP), BF16)
        one, zero = jnp.ones((), BF16), jnp.zeros((), BF16)
        for b in range(BAG):
            wanted = jnp.broadcast_to(ids[b : b + 1], (16, GROUP)).astype(BF16)
            total = total + jnp.where(jnp.tile(wanted, (SHARE // 16, 1)) == row, one, zero)
        columns = pl.ds(pl.multiple_of(where * GROUP, GROUP), GROUP)
        chip_counts[side, :, columns] = total

    def count_step(n, _):
        count_group(n)
        return 0

    for load in later_loads:
        load.wait()
    padding = jnp.zeros((1, 128 - COLUMN), jnp.int32)
    order = jnp.concatenate([placement_ref[...], padding - 1], axis=1)
    column_counts = jnp.concatenate([counts_ref[...], padding], axis=1).astype(F32)
    eye = iota((128, 128), 0) == iota((128, 128), 1)
    place_at = jnp.where(order == iota((128, 128), 0), iota((128, 128), 1).astype(F32), 0.0)
    position = jnp.sum(place_at, axis=1, keepdims=True)
    position_row = jnp.sum(jnp.where(eye, position, 0.0), axis=0, keepdims=True)
    start = jnp.sum(jnp.where(position_row < position, column_counts, 0.0), axis=1, keepdims=True)
    count = jnp.sum(jnp.where(eye, column_counts, 0.0), axis=1, keepdims=True)
    start_row = jnp.sum(jnp.where(eye, start, 0.0), axis=0, keepdims=True)
    end, end_row = start + count, start_row + column_counts
    first = (i * CAND).astype(F32)
    slot = first + iota((CAND, 1), 0, F32)
    slot_row = first + iota((1, CAND), 1, F32)
    member = jnp.where((slot >= start_row) & (slot < end_row), 1.0, 0.0).astype(BF16)
    member_turned = jnp.where((slot_row >= start) & (slot_row < end), 1.0, 0.0).astype(BF16)
    diagonal = iota((CAND, CAND), 0) == iota((CAND, CAND), 1)
    label = jnp.sum(jnp.where(diagonal, labels_ref[...].astype(F32), 0.0), axis=1, keepdims=True)

    item = item_ref[...]
    item_wide = item.astype(F32)
    item_pre = jnp.dot(item, w_hidden[E : 2 * E], preferred_element_type=F32) + bias_ref[...]

    lax.fori_loop(0, 2, count_step, 0)

    def wait_partial(s, _):
        arrived(partial_in, partial_recv, (k + s) % N_ROW)
        return 0

    lax.fori_loop(1, N_ROW, wait_partial, 0)
    pooled = jnp.sum(partial_in[...], axis=0)
    pooled_out[...] = pooled
    pooled_in[core, z] = pooled

    def send_pooled(s, _):
        z_copy(pooled_out, pooled_in.at[core, z], pooled_send, pooled_recv, alternate(N_Z - s, N_Z)).start()
        return 0

    def wait_ids(s, _):
        where = wrap(z + s, N_Z)
        arrived(ids_all, ids_recv, where)
        return 0

    def wait_pooled(s, _):
        where = wrap(z + s, N_Z)
        block = pooled_in.at[core, where]
        pltpu.make_async_copy(block, block, pooled_recv.at[where]).wait()
        return 0

    lax.fori_loop(1, N_Z, send_pooled, 0)
    pooled_column[...] = jnp.zeros_like(pooled_column)
    lax.fori_loop(1, N_Z, wait_ids, 0)
    lax.fori_loop(2, 12, count_step, 0)
    lax.fori_loop(1, N_Z, wait_pooled, 0)
    pooled_over = core_copy(pooled_in.at[core], pooled_in.at[core], 1)
    pooled_over.start()
    pooled_over.wait_recv()
    pooled_all = jnp.stack([pooled_in[0], pooled_in[1]], axis=1).reshape(N_DP, 8, 128)
    left, right = from_messages(pooled_all)
    pooled_column[:COLUMN, :128] = left.astype(BF16)
    pooled_column[:COLUMN, 128:] = right.astype(BF16)

    user_rows = jnp.dot(member, pooled_column[...], preferred_element_type=F32)
    user = user_rows.astype(BF16)
    both = (user_rows * item_wide).astype(BF16)
    pre = (
        item_pre
        + jnp.dot(user, w_hidden[:E], preferred_element_type=F32)
        + jnp.dot(both, w_hidden[2 * E :], preferred_element_type=F32)
    )
    sigma = jax.nn.sigmoid(pre)
    hidden = (pre * sigma).astype(BF16).astype(F32)
    w_out = w_out_ref[...].astype(F32).reshape(1, H)
    score = jnp.sum(hidden * w_out, axis=1, keepdims=True)
    dscore = loss_scale * (jax.nn.sigmoid(score) - label)
    slope = sigma * (1.0 + pre * (1.0 - sigma))
    dhidden = (dscore * w_out * slope).astype(BF16)
    dfeatures = lax.dot_general(dhidden, w_hidden[...], (((1,), (1,)), ((), ())), preferred_element_type=F32)
    user_grad = dfeatures[:, :E] + dfeatures[:, 2 * E :] * item_wide
    coarse = user_grad.astype(BF16)
    fine = (user_grad - coarse.astype(F32)).astype(BF16)
    column_grad = jnp.dot(member_turned, coarse, preferred_element_type=F32) + jnp.dot(
        member_turned, fine, preferred_element_type=F32
    )
    by_core = to_messages(column_grad[:COLUMN]).reshape(N_Z, 2, 8, 128)
    grad_out[0] = by_core[:, 0]
    grad_out[1] = by_core[:, 1]

    grad_over = core_copy(grad_out.at[1 - core], grad_core, 2)
    grad_over.start()
    item_grad_ref[...] = (dfeatures[:, E : 2 * E] + dfeatures[:, 2 * E :] * user_rows).astype(BF16)
    item_store = pltpu.make_async_copy(item_grad_ref, item_grad_hbm, store_sem.at[0])
    item_store.start()
    grad_over.wait_recv()
    grad_pair[...] = grad_out[core] + grad_core[...]

    def send_grad(s, _):
        step = alternate(N_Z - s, N_Z)
        z_copy(grad_pair.at[wrap(z + step, N_Z)], grad_in.at[z], grad_send, grad_recv, step).start()
        return 0

    def wait_grad(s, _):
        arrived(grad_in, grad_recv, wrap(z + s, N_Z))
        return 0

    lax.fori_loop(1, N_Z, send_grad, 0)
    grad_in[z] = grad_pair[z]
    lax.fori_loop(12, 22, count_step, 0)
    lax.fori_loop(1, N_Z, wait_grad, 0)
    request_grad = jnp.sum(grad_in[...], axis=0)
    request_out[...] = request_grad
    request_in[y] = request_grad

    def y_copy(s):
        return pltpu.make_async_remote_copy(
            src_ref=request_out,
            dst_ref=request_in.at[y],
            send_sem=request_send.at[s],
            recv_sem=request_recv.at[y],
            device_id=(i, (k + s * N_X) % N_ROW),
            device_id_type=MESH,
        )

    for s in (4, 3, 5, 2, 6, 1, 7):
        y_copy(s).start()
    lax.fori_loop(22, 24, count_step, 0)
    for s in range(1, N_Y):
        arrived(request_in, request_recv, (y + s) % N_Y)
    left, right = from_messages(request_in[...])
    own_rows = pl.ds(pl.multiple_of(x * QUARTER, QUARTER), QUARTER)
    all_grads[z, own_rows, :128] = left.astype(BF16)
    all_grads[z, own_rows, 128:] = right.astype(BF16)

    def quarter(where, which):
        return all_grads.at[where, pl.ds(pl.multiple_of(which * QUARTER, QUARTER), QUARTER)]

    def send_z(s, _):
        z_copy(quarter(z, x), quarter(z, x), z_send, z_recv, alternate(s, N_Z)).start()
        return 0

    def x_copy(where, which, s):
        return pltpu.make_async_remote_copy(
            src_ref=quarter(where, which),
            dst_ref=quarter(where, which),
            send_sem=x_send.at[where, s],
            recv_sem=x_recv.at[where, which],
            device_id=(i, y * N_X + (x + s) % N_X),
            device_id_type=MESH,
        )

    lax.fori_loop(1, N_Z, send_z, 0)
    for step in (2, 1, 3):
        x_copy(z, x, step).start()

    def pass_on(s, _):
        where = wrap(z + alternate(s, N_Z), N_Z)
        block = quarter(where, x)
        pltpu.make_async_copy(block, block, z_recv.at[where]).wait()
        for step in (2, 1, 3):
            x_copy(where, x, step).start()
        return 0

    lax.fori_loop(1, N_Z, pass_on, 0)

    def drain_z(s, _):
        z_copy(ids_all.at[z], ids_all.at[z], ids_send, ids_recv, s).wait_send()
        z_copy(pooled_out, pooled_in.at[core, z], pooled_send, pooled_recv, s).wait_send()
        z_copy(grad_pair.at[0], grad_in.at[z], grad_send, grad_recv, s).wait_send()
        z_copy(quarter(z, x), quarter(z, x), z_send, z_recv, s).wait_send()
        return 0

    for s in range(1, N_Y):
        y_copy(s).wait_send()
    for step in ROW_STEPS:
        row_copy(partial_out.at[0], partial_in.at[k], partial_send, partial_recv, step).wait_send()
    lax.fori_loop(1, N_Z, drain_z, 0)
    pooled_over.wait_send()
    grad_over.wait_send()

    def product(where, side):
        columns = pl.ds(pl.multiple_of(where * GROUP, GROUP), GROUP)
        return jnp.dot(chip_counts[side, :, columns], all_grads[where], preferred_element_type=F32)

    def wait_x(s):
        where = wrap(z + alternate(s, N_Z), N_Z)
        for step in range(1, N_X):
            which = (x + step) % N_X
            block = quarter(where, which)
            pltpu.make_async_copy(block, block, x_recv.at[where, which]).wait()
        return where

    def add_group(s, _):
        where = wait_x(s)
        for side in range(2):
            parts[side] = parts[side] + product(where, side)
        return 0

    parts[...] = jnp.zeros_like(parts)
    lax.fori_loop(0, N_Z - 1, add_group, 0)
    last = wait_x(N_Z - 1)
    part_out[...] = (parts[1 - core] + product(last, 1 - core)).astype(BF16)
    part_over = core_copy(part_out, part_in, 3)
    part_over.start()

    def drain_x(where, _):
        for step in range(1, N_X):
            x_copy(where, x, step).wait_send()
        return 0

    lax.fori_loop(0, N_Z, drain_x, 0)
    own_part = parts[core] + product(last, core)
    part_over.wait_recv()
    table_grad_ref[...] = own_part + part_in[...].astype(F32)
    table_store = pltpu.make_async_copy(table_grad_ref, table_grad_hbm, store_sem.at[1])
    table_store.start()

    part_over.wait_send()
    table_store.wait()
    item_store.wait()


def hand_over(table_grad_hbm, item_grad_hbm, table_grad_out, item_grad_out, table_grad, item_grad, sem):
    parts = []
    for n, (source, held, target) in enumerate(
        [(table_grad_hbm, table_grad, table_grad_out), (item_grad_hbm, item_grad, item_grad_out)]
    ):
        for part in range(2):
            rows = pl.ds(part * 128, 128)
            parts.append(
                (
                    pltpu.make_async_copy(source.at[rows], held.at[rows], sem.at[0, n, part]),
                    pltpu.make_async_copy(held.at[rows], target.at[rows], sem.at[1, n, part]),
                )
            )
    for load, _ in parts:
        load.start()
    for load, store in parts:
        load.wait()
        store.start()
    for _, store in parts:
        store.wait()


def per_device(user_table, user_ids, item_features, counts, placement, labels, w_hidden, bias, w_out):
    vmem = pl.BlockSpec(memory_space=pltpu.VMEM)
    hbm = pl.BlockSpec(memory_space=pl.ANY)
    dma = pltpu.SemaphoreType.DMA
    outs = (jax.ShapeDtypeStruct((SHARE, E), F32), jax.ShapeDtypeStruct((CAND, E), BF16))
    grads = pl.pallas_call(
        kernel,
        out_shape=outs,
        in_specs=[hbm] * 8 + [vmem],
        out_specs=(hbm, hbm),
        scratch_shapes=[
            pltpu.VMEM((SHARE, E), F32),
            pltpu.VMEM((CAND, E), BF16),
            pltpu.VMEM((ROWS, E), BF16),
            pltpu.VMEM((3 * E, H), BF16),
            pltpu.VMEM((BAG, GROUP), jnp.int32),
            pltpu.VMEM((CAND, E), BF16),
            pltpu.VMEM((1, COLUMN), jnp.int32),
            pltpu.VMEM((1, COLUMN), jnp.int32),
            pltpu.VMEM((1, CAND), jnp.int32),
            pltpu.VMEM((1, H), F32),
            pltpu.VMEM((GROUP, ROWS), BF16),
            pltpu.VMEM((N_ROW, 8, 128), F32),
            pltpu.VMEM((N_ROW, 8, 128), F32),
            pltpu.VMEM((8, 128), F32),
            pltpu.VMEM((2, N_Z, 8, 128), F32),
            pltpu.VMEM((128, E), BF16),
            pltpu.VMEM((2, N_Z, 8, 128), F32),
            pltpu.VMEM((N_Z, 8, 128), F32),
            pltpu.VMEM((N_Z, 8, 128), F32),
            pltpu.VMEM((N_Z, 8, 128), F32),
            pltpu.VMEM((8, 128), F32),
            pltpu.VMEM((N_Y, 8, 128), F32),
            pltpu.VMEM((N_Z, BAG, GROUP), jnp.int16),
            pltpu.VMEM((2, SHARE, N_Z * GROUP), BF16),
            pltpu.VMEM((N_Z, GROUP, E), BF16),
            pltpu.VMEM((2, SHARE, E), F32),
            pltpu.VMEM((SHARE, E), BF16),
            pltpu.VMEM((SHARE, E), BF16),
            dma((8,)),
            dma((2,)),
            dma((N_Z,)),
            dma((N_Z,)),
            dma((N_ROW,)),
            dma((N_ROW,)),
            dma((N_Z,)),
            dma((N_Z,)),
            dma((N_Z,)),
            dma((N_Z,)),
            dma((N_Y,)),
            dma((N_Y,)),
            dma((N_Z,)),
            dma((N_Z,)),
            dma((N_Z, N_X)),
            dma((N_Z, N_X)),
            dma((4,)),
            dma((4,)),
        ],
        compiler_params=pltpu.CompilerParams(
            collective_id=0, has_side_effects=True, vmem_limit_bytes=60 * 1024 * 1024
        ),
    )(
        user_table,
        user_ids.T,
        item_features,
        counts,
        placement,
        labels.reshape(1, CAND),
        w_hidden,
        bias.reshape(1, H),
        w_out,
    )
    return pl.pallas_call(
        hand_over,
        out_shape=outs,
        in_specs=[hbm] * 2,
        out_specs=(hbm, hbm),
        scratch_shapes=[pltpu.VMEM((SHARE, E), F32), pltpu.VMEM((CAND, E), BF16), dma((2, 2, 2))],
        compiler_params=pltpu.CompilerParams(vmem_limit_bytes=60 * 1024 * 1024),
    )(*grads)


def solution(mesh):
    return jax.shard_map(
        per_device,
        mesh=mesh,
        in_specs=(
            P("row", None),
            P("dp", None),
            P(("dp", "row"), None),
            P("row", None),
            P("row", None),
            P(("dp", "row")),
            P(),
            P(),
            P(),
        ),
        out_specs=(P(("row", "dp"), None), P(("dp", "row"), None)),
        check_vma=False,
    )
```
